32 devices in a mesh: ctx: 4 (over y, x), exp: 8 (over z, core).
Axes of the slice: x: 2, y: 2, z: 4, core: 2. Of those that a mesh axis runs over, the one named last changes fastest.
Arguments:
- moe_input: bfloat16 [1024, 3584], P('exp', 'ctx'), may hold values from -6 to 6
- moe_grad: bfloat16 [1024, 3584], P('exp', 'ctx'), may hold values from -6 to 6
- routes: int32 [1024, 8], P('exp'), may hold values from 0 to 15, all different within a row; in each aligned block of 128 rows (0 to 127, 128 to 255, ...) at most 80 rows name the same one
- gates: float32 [1024, 8], P('exp'), may hold values from 0.05 to 0.5
- w_gate: bfloat16 [16, 3584, 1024], P('exp', 'ctx'), may hold values from -0.09375 to 0.09375
- w_up: bfloat16 [16, 3584, 1024], P('exp', 'ctx'), may hold values from -0.09375 to 0.09375
- w_down: bfloat16 [16, 1024, 3584], P('exp', None, 'ctx'), may hold values from -0.1875 to 0.1875
- queries: bfloat16 [512, 9216], P('ctx', 'exp'), may hold values from -16 to 16
- out_grad: bfloat16 [512, 8192], P('ctx', 'exp'), may hold values from -6 to 6
- positions: int32 [512], P('ctx'), may hold values from 0 to 1023, as said below
- latents: bfloat16 [1024, 576], P('ctx'), may hold values from -6 to 6
Outputs:
- moe_input_grad: bfloat16 [1024, 3584], P('exp', 'ctx')
- query_grad: bfloat16 [512, 9216], P('ctx', 'exp')
- latent_grad: float32 [1024, 576], P(('ctx', 'exp'))
The draws below stay inside these ranges and needn't reach their ends.
Inputs may be any that keep to these rules, and one draw needn't show every extreme that they name: `routes`: each row names 8 different experts; among the 128 rows of one index of exp no expert is named more than 80 times, and in some such block one is named exactly 80 times. Row i lies within the keys of its own context shard, (i // 128) * 256 <= positions[i] < (i // 128 + 1) * 256; the first row of each shard sits at the shard's first key and the last row at its last key.
All inputs are finite; a program needn't handle non-finite values.
Results may differ from the reference program's by a relative error of at most 0.018.
Values may be sent and summed in bfloat16 or wider, within the bound.
No kernel may reach another device: no remote copies, remote signals or barrier semaphores. Data moves between devices by JAX's collectives and lax.ppermute only.
A program may use at most 128 MiB of HBM per device.

```python
import math
import jax
import jax.numpy as jnp
import numpy as np
from jax import lax

D = 3584
HID = 1024
TOP = 8
TOK_DEV = 128
LAT = 576
VAL = 512
QROWS = 128
KEY_DEV = 256
EXPERTS = 16
CAP = 80
TOKENS = 1024
DQ = 896
HEADS = 16
QALL = 512
KEYS = 1024
N_EXP = 8


def latent_table(key):
    base = jax.random.fold_in(key, 11)
    table = jax.random.truncated_normal(base, -4.0, 4.0, (KEYS, LAT), jnp.float32)
    return table


def draw_latents(key, part):
    return latent_table(key).astype(jnp.bfloat16)


def draw_queries(key, part):
    base = jax.random.fold_in(key, 23)
    values = jax.random.truncated_normal(base, -4.0, 4.0, (QALL, HEADS * LAT), jnp.float32)
    return values.astype(jnp.bfloat16)


def draw_positions(key, part):
    row_ids = jnp.arange(QALL, dtype=jnp.int32)
    shard = row_ids // QROWS
    inner = row_ids % QROWS
    offset = jax.random.randint(jax.random.fold_in(key, 31), (QALL,), 0, KEY_DEV, dtype=jnp.int32)
    offset = jnp.where(inner == 0, 0, offset)
    offset = jnp.where(inner == QROWS - 1, KEY_DEV - 1, offset)
    return (shard * KEY_DEV + offset).astype(jnp.int32)


def block_scale(stream_key, shape, pieces, smallest, largest):
    level, own = 1.0, jax.random.fold_in(stream_key, 6)
    for axis_at, blocks in pieces:
        draws = jnp.exp(jax.random.uniform(jax.random.fold_in(own, axis_at), (blocks,), jnp.float32, smallest / len(pieces), largest / len(pieces)))
        level = level * jnp.repeat(draws, shape[axis_at] // blocks).reshape([-1 if axis == axis_at else 1 for axis in range(len(shape))])
    return level


def routed_block(rng, own, number, rows, amount, top, reach, skew):
    sequence = jax.random.permutation(rng, amount)
    crowded, usual = shares(amount, rows * top, reach, skew, True), shares(amount, rows * top, reach, skew, False)
    places = jnp.arange(amount)

    def named(tallies, turn):
        used = int((tallies > 0).sum())
        fixed = max(1, used // 4)
        moved = fixed + (places - fixed + turn * (used - fixed)) % max(1, amount - fixed)
        return jnp.zeros((amount,), jnp.int32).at[sequence[jnp.where(places < fixed, places, moved)]].set(jnp.asarray(tallies, jnp.int32))

    tallies = jnp.where(number % 4 == 0, named(crowded, number // 4), named(usual, number - number // 4 - 1))
    mixed = jax.random.permutation(jax.random.fold_in(own, 3), amount)
    source_of, sink = mixed[0:amount // 2 * 2:2], mixed[1:amount // 2 * 2:2]
    margin = jnp.minimum(tallies[source_of] - 1, reach - tallies[sink]) // 2
    margin = jnp.where((source_of == sequence[0]) | (sink == sequence[0]) | (tallies[sink] == 0), 0, jnp.maximum(margin, 0))
    moved = jax.random.randint(jax.random.fold_in(own, 4), (amount // 2,), 0, 1 << 20) % (margin + 1)
    tallies = tallies.at[source_of].add(-moved).at[sink].add(moved)
    members = jnp.searchsorted(jnp.cumsum(tallies), jnp.arange(rows * top), side="right").astype(jnp.int32)
    table = members.reshape(top, rows).T
    table = table[jax.random.permutation(jax.random.fold_in(own, 1), rows)]
    turn = jax.random.randint(jax.random.fold_in(own, 2), (rows, 1), 0, top)
    return jnp.take_along_axis(table, (jnp.arange(top)[None, :] + turn) % top, axis=1)


def shares(number_of, total, limit, skew, full):
    weights = [(1 << 20) // math.isqrt(rank ** skew) + 1 for rank in range(1, number_of + 1)]
    largest = limit if full else min(limit, max(-(-total // number_of), total * weights[0] // sum(weights)))
    least = 1 if total - largest >= number_of - 1 else 0
    given, rest = [largest] + [least] * (number_of - 1), total - largest - least * (number_of - 1)
    while rest > 0:
        candidates = [i for i in range(1, number_of) if given[i] < largest] or [i for i in range(1, number_of) if given[i] < limit]
        pool, remaining = sum([weights[i] for i in candidates]), rest
        for i in candidates:
            addition = min(limit - given[i], max(1, remaining * weights[i] // pool), rest)
            given[i] = given[i] + addition
            rest = rest - addition
    return np.array(given)


def scatter_about(rng, extent, spread, bound, pieces=(), kind=jnp.bfloat16):
    gain = block_scale(rng, extent, pieces, -0.22, 0.18) if pieces else 1.0
    array = jax.random.normal(rng, extent, jnp.float32) * spread * gain
    return jnp.minimum(jnp.maximum(array, -bound), bound).astype(kind)


def setup_inputs(seed: int = 0) -> dict:
    key_of = jax.random.split(jax.random.key(seed), 12)
    moe_input = scatter_about(key_of[0], (TOKENS, D), 1.0, 6.0, ((0, 8), (1, 4)))
    moe_grad = scatter_about(key_of[1], (TOKENS, D), 1.0, 6.0, ((0, 8), (1, 4)))
    routes_keys = jax.random.split(jax.random.fold_in(key_of[2], 1), TOKENS // TOK_DEV)
    routes_turns = jax.random.permutation(jax.random.fold_in(key_of[2], 3), TOKENS // TOK_DEV)
    routes = jax.vmap(lambda own, number: routed_block(jax.random.fold_in(key_of[2], 2), own, number, TOK_DEV, EXPERTS, TOP, CAP, 2))(routes_keys, routes_turns).reshape((TOKENS, TOP))
    gates = jnp.clip(0.05 + 0.45 * jax.random.uniform(key_of[3], (TOKENS, TOP), jnp.float32) ** block_scale(key_of[3], (TOKENS, TOP), ((0, 8),), -0.2, 0.2), 0.05, 0.5)
    w_gate = scatter_about(key_of[4], (EXPERTS, D, HID), D ** -0.5, 0.09375, ((0, 8), (1, 4)))
    w_up = scatter_about(key_of[5], (EXPERTS, D, HID), D ** -0.5, 0.09375, ((0, 8), (1, 4)))
    w_down = scatter_about(key_of[6], (EXPERTS, HID, D), HID ** -0.5, 0.1875, ((0, 8), (2, 4)))
    queries = draw_queries(jax.random.fold_in(key_of[11], 71), 0)
    out_grad = scatter_about(key_of[8], (QALL, HEADS * VAL), 1.0, 6.0, ((0, 4), (1, 8)))
    positions = draw_positions(jax.random.fold_in(key_of[11], 71), 0)
    latents = draw_latents(jax.random.fold_in(key_of[11], 71), 0)
    return dict(moe_input=moe_input, moe_grad=moe_grad, routes=routes, gates=gates, w_gate=w_gate, w_up=w_up, w_down=w_down, queries=queries, out_grad=out_grad, positions=positions, latents=latents)


SCORE_SCALE = 192.0 ** -0.5
MASKED = -1.0e30


def swiglu_back(gate_pre, up_pre, hidden_grad):
    sigma = jax.nn.sigmoid(gate_pre)
    gate_back = hidden_grad * up_pre * sigma * (1.0 + gate_pre * (1.0 - sigma))
    up_back = hidden_grad * gate_pre * sigma
    return gate_back.astype(jnp.bfloat16), up_back.astype(jnp.bfloat16)


def rounded_blocks(left, right):
    partial_sums = jnp.einsum("mcd,cdh->mch", left, right)
    lowered = lax.optimization_barrier(partial_sums.astype(jnp.bfloat16))
    return jnp.sum(lowered.astype(jnp.float32), axis=1)


def expert_ranks(block_routes):
    onehot = (block_routes[:, None] == jnp.arange(EXPERTS, dtype=jnp.int32)[None, :]).astype(jnp.int32)
    before = jnp.cumsum(onehot, axis=0) - onehot
    return jnp.sum(before * onehot, axis=1).astype(jnp.int32)


def expert_part(moe_input, moe_grad, routes, gates, w_gate, w_up, w_down):
    per_block = TOK_DEV * TOP
    block_routes = routes.reshape(N_EXP, per_block).astype(jnp.int32)
    slots = lax.map(expert_ranks, block_routes)
    column = (jnp.arange(N_EXP, dtype=jnp.int32)[:, None] * CAP + slots).astype(jnp.int32)
    route_ids = jnp.arange(TOKENS * TOP, dtype=jnp.int32).reshape(N_EXP, per_block)
    table = jnp.full((EXPERTS, N_EXP * CAP), -1, jnp.int32).at[block_routes, column].set(route_ids)
    flat_gates = gates.reshape(-1)
    blocks = D // DQ

    def expert_step(carry, packed):
        row_table, gate_weight, up_weight, down_weight = packed
        valid = row_table >= 0
        route_index = jnp.where(valid, row_table, 0).astype(jnp.int32)
        token_index = (route_index // TOP).astype(jnp.int32)
        rows_in = moe_input[token_index].astype(jnp.float32).reshape(-1, blocks, DQ)
        rows_grad = moe_grad[token_index].astype(jnp.float32).reshape(-1, blocks, DQ)
        gate_pre = rounded_blocks(rows_in, gate_weight.astype(jnp.float32).reshape(blocks, DQ, HID))
        up_pre = rounded_blocks(rows_in, up_weight.astype(jnp.float32).reshape(blocks, DQ, HID))
        down_blocks = jnp.transpose(down_weight.astype(jnp.float32).reshape(HID, blocks, DQ), (1, 2, 0))
        hidden_grad = rounded_blocks(rows_grad, down_blocks)
        gate_back, up_back = swiglu_back(gate_pre, up_pre, hidden_grad)
        route_grad = jnp.dot(gate_back, gate_weight.T, preferred_element_type=jnp.float32)
        route_grad = route_grad + jnp.dot(up_back, up_weight.T, preferred_element_type=jnp.float32)
        lowered = lax.optimization_barrier(route_grad.astype(jnp.bfloat16)).astype(jnp.float32)
        scaled = jnp.where(valid[:, None], flat_gates[route_index][:, None] * lowered, 0.0)
        return carry.at[token_index].add(scaled), None

    total, _ = lax.scan(expert_step, jnp.zeros((TOKENS, D), jnp.float32), (table, w_gate, w_up, w_down))
    return total.astype(jnp.bfloat16)


def attention_part(queries, out_grad, positions, latents):
    query_heads = jnp.transpose(queries.reshape(QALL, HEADS, LAT), (1, 0, 2))
    grad_heads = jnp.transpose(out_grad.reshape(QALL, HEADS, VAL), (1, 0, 2))
    visible = jnp.arange(KEYS, dtype=jnp.int32)[None, :] <= positions[:, None]
    values = latents[:, :VAL]

    def head_step(carry, packed):
        query_one, grad_one = packed
        scores = jnp.dot(query_one, latents.T, preferred_element_type=jnp.float32) * SCORE_SCALE
        scores = jnp.where(visible, scores, MASKED)
        peak = jnp.max(scores, axis=1, keepdims=True)
        raw = jnp.where(visible, jnp.exp(scores - peak), 0.0)
        attend = raw / jnp.sum(raw, axis=1, keepdims=True)
        value_dot = jnp.dot(grad_one, values.T, preferred_element_type=jnp.float32)
        row_dot = jnp.sum(attend * value_dot, axis=1, keepdims=True)
        score_grad = (attend * (value_dot - row_dot)).astype(jnp.bfloat16)
        query_grad = jnp.dot(score_grad, latents, preferred_element_type=jnp.float32) * SCORE_SCALE
        key_grad = jnp.dot(score_grad.T, query_one, preferred_element_type=jnp.float32) * SCORE_SCALE
        value_grad = jnp.dot(attend.astype(jnp.bfloat16).T, grad_one, preferred_element_type=jnp.float32)
        carry = carry + key_grad + jnp.pad(value_grad, ((0, 0), (0, LAT - VAL)))
        return carry, query_grad.astype(jnp.bfloat16)

    latent_grad, query_grads = lax.scan(head_step, jnp.zeros((KEYS, LAT), jnp.float32), (query_heads, grad_heads))
    query_grad = jnp.transpose(query_grads, (1, 0, 2)).reshape(QALL, HEADS * LAT)
    return query_grad, latent_grad


def reference(moe_input, moe_grad, routes, gates, w_gate, w_up, w_down, queries, out_grad, positions, latents):
    moe_input_grad = expert_part(moe_input, moe_grad, routes, gates, w_gate, w_up, w_down)
    query_grad, latent_grad = attention_part(queries, out_grad, positions, latents)
    return (moe_input_grad, query_grad, latent_grad)
```

```python
import functools

import jax
import jax.numpy as jnp
from jax import lax
from jax.experimental import pallas as pl
from jax.experimental.pallas import tpu as pltpu
from jax.sharding import PartitionSpec as P

SCORE_SCALE = 192.0 ** (-0.5)
MASKED = -1e30
BF16 = jnp.bfloat16
F32 = jnp.float32
META = 128
VMEM_LIMIT = 48 * 1024 * 1024


def swiglu_back(gate_pre, up_pre, hidden_grad):
    sigma = jax.nn.sigmoid(gate_pre)
    gate_back = hidden_grad * up_pre * sigma * (1.0 + gate_pre * (1.0 - sigma))
    up_back = hidden_grad * gate_pre * sigma
    return (gate_back.astype(BF16), up_back.astype(BF16))


def shift(value, axis, bits):
    count = lax.axis_size(axis)
    return lax.ppermute(value, axis, [(i, i ^ bits) for i in range(count)])


def dot(left, right):
    return jnp.dot(left, right, preferred_element_type=F32)


def dot_t(left, right):
    return lax.dot_general(left, right, (((1,), (1,)), ((), ())), preferred_element_type=F32)


def pack_kernel(experts, routes_ref, gates_ref, input_ref, grad_ref, out_ref):
    rows, width = input_ref.shape
    out_ref[:, :width] = input_ref[...]
    out_ref[:, width : 2 * width] = grad_ref[...]
    lane = lax.broadcasted_iota(jnp.int32, (rows, META), 1)
    expert = lane % experts
    section = lane // experts
    gate = jnp.zeros((rows, META), F32)
    named = jnp.zeros((rows, META), F32)
    for k in range(routes_ref.shape[1]):
        hit = routes_ref[:, k : k + 1] == expert
        gate = gate + jnp.where(hit, gates_ref[:, k : k + 1], 0.0)
        named = named + jnp.where(hit, 1.0, 0.0)
    low = lax.broadcasted_iota(jnp.int32, (rows, rows), 0)
    high = lax.broadcasted_iota(jnp.int32, (rows, rows), 1)
    before = jnp.where(high < low, 1.0, 0.0).astype(BF16)
    slot = jnp.where(named > 0.0, dot(before, named.astype(BF16)), -1.0)
    gate_high = gate.astype(BF16).astype(F32)
    meta = jnp.where(section == 0, gate_high, jnp.where(section == 1, gate - gate_high, slot))
    out_ref[:, 2 * width :] = meta.astype(BF16)


def pack_tokens(moe_input, moe_grad, routes, gates, experts):
    rows, width = moe_input.shape
    return pl.pallas_call(
        functools.partial(pack_kernel, experts),
        out_shape=jax.ShapeDtypeStruct((rows, 2 * width + META), BF16),
        compiler_params=pltpu.CompilerParams(vmem_limit_bytes=VMEM_LIMIT),
        cost_estimate=pl.CostEstimate(
            flops=2 * rows * rows * META, bytes_accessed=8 * rows * width, transcendentals=0
        ),
        name="pack_tokens",
    )(routes, gates, moe_input, moe_grad)


def fill_rows(plan_ref, expert, experts, capacity, token_refs, rows_ref):
    width = rows_ref.shape[-1]
    tokens = token_refs[0].shape[0]
    lane = lax.broadcasted_iota(jnp.int32, (16, META), 1)
    pick = jnp.where(lane == 2 * experts + plan_ref[0] + expert, 1.0, 0.0).astype(BF16)
    for b, token_ref in enumerate(token_refs):
        slot_of = dot_t(pick, token_ref[:, 2 * width :])[0:1, :].astype(jnp.int32)
        slot = lax.broadcasted_iota(jnp.int32, (capacity, tokens), 0)
        chosen = jnp.where(slot == slot_of, 1.0, 0.0).astype(BF16)
        part = pl.ds(b * capacity, capacity)
        rows_ref[expert, 0, part, :] = dot(chosen, token_ref[:, :width]).astype(BF16)
        rows_ref[expert, 1, part, :] = dot(chosen, token_ref[:, width : 2 * width]).astype(BF16)


def products_kernel(blocks, experts, capacity, plan_ref, *refs):
    expert, piece = pl.program_id(0), pl.program_id(1)
    if blocks:
        token_refs, refs = refs[:blocks], refs[blocks:]
        gate_ref, up_ref, down_ref, first_ref, second_ref, rows_ref = refs

        @pl.when(piece == 0)
        def _():
            fill_rows(plan_ref, expert, experts, capacity, token_refs, rows_ref)
    else:
        rows_ref, gate_ref, up_ref, down_ref, first_ref, second_ref = refs
    rows_in, rows_grad = rows_ref[expert, 0], rows_ref[expert, 1]
    gate = dot(rows_in, gate_ref[0]).astype(BF16)
    up = dot(rows_in, up_ref[0]).astype(BF16)
    down = dot_t(rows_grad, down_ref[0]).astype(BF16)

    def store(out_ref):
        out_ref[0, piece] = gate
        out_ref[1, piece] = up
        out_ref[2, piece] = down

    pl.when(expert == 0)(lambda: store(first_ref))
    pl.when(expert == 1)(lambda: store(second_ref))


def products(plan, base, tokens, rows, w_gate, w_up, w_down, capacity, experts):
    local, width, hidden = w_gate.shape
    quarter = hidden // 4
    blocks = len(tokens)
    slots = blocks * capacity if blocks else rows.shape[2]

    def column(e, j, plan_ref):
        return (e, 0, plan_ref[base + 2 * e + j])

    def line(e, j, plan_ref):
        return (e, plan_ref[base + 2 * e + j], 0)

    whole = pl.BlockSpec(memory_space=pltpu.VMEM)
    part_shape = jax.ShapeDtypeStruct((3, 2, slots, quarter), BF16)
    rows_shape = jax.ShapeDtypeStruct((local, 2, slots, width), BF16)

    def fixed(shape):
        return pl.BlockSpec(shape, lambda e, j, plan_ref: (0,) * len(shape))

    head = list(tokens) if blocks else [rows]
    out_shape = [part_shape, part_shape] + ([rows_shape] if blocks else [])
    return pl.pallas_call(
        functools.partial(products_kernel, blocks, experts, capacity),
        out_shape=out_shape,
        grid_spec=pltpu.PrefetchScalarGridSpec(
            num_scalar_prefetch=1,
            grid=(local, 2),
            in_specs=[fixed(a.shape) for a in head]
            + [
                pl.BlockSpec((1, width, quarter), column),
                pl.BlockSpec((1, width, quarter), column),
                pl.BlockSpec((1, quarter, width), line),
            ],
            out_specs=[fixed(s.shape) for s in out_shape],
        ),
        compiler_params=pltpu.CompilerParams(vmem_limit_bytes=VMEM_LIMIT),
        cost_estimate=pl.CostEstimate(
            flops=2 * local * 3 * slots * width * hidden // 2,
            bytes_accessed=2 * local * 3 * width * hidden // 2 + 4 * local * slots * width,
            transcendentals=0,
        ),
        name="products",
    )(plan, *head, w_gate, w_up, w_down)


def route_kernel(blocks, experts, capacity, plan_ref, *refs):
    expert, piece = pl.program_id(0), pl.program_id(1)
    meta_refs, refs = refs[:blocks], refs[blocks:]
    piece_refs, refs = refs[:8], refs[8:]
    gate_ref, up_ref = refs[:2]
    out_refs = refs[2 : 2 + blocks]
    route_ref, total_ref = refs[2 + blocks :]
    tokens = meta_refs[0].shape[0]

    def add(back_ref, first):
        value = dot_t(back_ref[0], gate_ref[0]) + dot_t(back_ref[1], up_ref[0])
        if first:
            route_ref[...] = value
        else:
            route_ref[...] += value

    for e in range(2):
        for p in range(4):
            pl.when((expert == e) & (piece == p))(
                functools.partial(add, piece_refs[4 * e + p], p == 0)
            )

    @pl.when(piece == 3)
    def _():
        row = lax.broadcasted_iota(jnp.int32, (META, META), 0)
        lane = lax.broadcasted_iota(jnp.int32, (META, META), 1)
        pick = jnp.where(lane == row * experts + plan_ref[0] + expert, 1.0, 0.0).astype(BF16)
        slot = lax.broadcasted_iota(jnp.int32, (tokens, capacity), 1)
        for b in range(blocks):
            found = dot_t(meta_refs[b][...], pick)
            mine = found[:, 2:3].astype(jnp.int32) == slot
            high = jnp.where(mine, found[:, 0:1], 0.0).astype(BF16)
            low = jnp.where(mine, found[:, 1:2], 0.0).astype(BF16)
            route = route_ref[pl.ds(b * capacity, capacity), :].astype(BF16)
            value = dot(high, route) + dot(low, route)

            @pl.when(expert == 0)
            def _():
                total_ref[b] = value

            @pl.when(expert == 1)
            def _():
                out_refs[b][...] = (total_ref[b] + value).astype(out_refs[b].dtype)


def route_sums(plan, base, tokens, pieces, w_gate, w_up, capacity, experts, out_type):
    local, width, hidden = w_gate.shape
    quarter = hidden // 4
    blocks = len(tokens)
    slots = blocks * capacity
    count = tokens[0].shape[0]
    meta_at = 2 * width // META

    def column(e, p, plan_ref):
        return (e, 0, plan_ref[base + 4 * e + p])

    def fixed(shape):
        return pl.BlockSpec(shape, lambda e, p, plan_ref: (0,) * len(shape))

    return pl.pallas_call(
        functools.partial(route_kernel, blocks, experts, capacity),
        out_shape=[jax.ShapeDtypeStruct((count, width), out_type)] * blocks,
        grid_spec=pltpu.PrefetchScalarGridSpec(
            num_scalar_prefetch=1,
            grid=(local, 4),
            in_specs=[pl.BlockSpec((count, META), lambda e, p, plan_ref: (0, meta_at))] * blocks
            + [fixed(a.shape) for a in pieces]
            + [pl.BlockSpec((1, width, quarter), column)] * 2,
            out_specs=[fixed((count, width))] * blocks,
            scratch_shapes=[pltpu.VMEM((slots, width), F32), pltpu.VMEM((blocks, count, width), F32)],
        ),
        compiler_params=pltpu.CompilerParams(vmem_limit_bytes=VMEM_LIMIT),
        cost_estimate=pl.CostEstimate(
            flops=2 * local * 2 * slots * width * hidden,
            bytes_accessed=2 * local * 2 * width * hidden + 4 * local * slots * hidden,
            transcendentals=0,
        ),
        name="route_sums",
    )(plan, *tokens, *pieces, w_gate, w_up)


def chunk_layer(plan, tokens, w_gate, w_up, w_down, capacity, experts, out_type):
    sent = products(plan, 1, tokens, None, w_gate, w_up, w_down, capacity, experts)
    rows = sent[2]
    kept = products(plan, 5, [], rows, w_gate, w_up, w_down, capacity, experts)
    pieces = []
    for e, (near, far) in enumerate(((1, 2), (2, 1))):
        got = shift(sent[e], "ctx", near)
        half = got.astype(F32) + kept[e].astype(F32)
        other = shift(half[:, 0].astype(BF16), "ctx", far)
        full = half[:, 1] + other.astype(F32)
        own = jnp.stack(swiglu_back(full[0], full[1], full[2]))
        from_far = shift(own, "ctx", far)
        from_near = shift(own, "ctx", near)
        from_both = shift(from_far, "ctx", near)
        pieces += [own, from_far, from_near, from_both]
    return route_sums(plan, 9, tokens, pieces, w_gate, w_up, capacity, experts, out_type)


def near_expert_layer(moe_input, moe_grad, routes, gates, w_gate, w_up, w_down):
    tok_rows = moe_input.shape[0]
    fanout = routes.shape[1]
    local = w_gate.shape[0]
    exp_count = lax.axis_size("exp")
    experts = local * exp_count
    capacity = tok_rows * fanout // experts * 5 // 4
    ctx = lax.axis_index("ctx")
    x, y = ctx % 2, ctx // 2
    plan = jnp.stack(
        [
            lax.axis_index("exp") * local,
            (1 - x) * 2 + 1 - y,
            (1 - x) * 2 + y,
            (1 - y) * 2 + 1 - x,
            (1 - y) * 2 + x,
            x * 2 + 1 - y,
            x * 2 + y,
            y * 2 + 1 - x,
            y * 2 + x,
            x * 2 + y,
            x * 2 + 1 - y,
            (1 - x) * 2 + y,
            (1 - x) * 2 + 1 - y,
            y * 2 + x,
            y * 2 + 1 - x,
            (1 - y) * 2 + x,
            (1 - y) * 2 + 1 - x,
        ]
    ).astype(jnp.int32)
    own = pack_tokens(moe_input, moe_grad, routes, gates, experts)
    layer = functools.partial(
        chunk_layer, plan, w_gate=w_gate, w_up=w_up, w_down=w_down, capacity=capacity, experts=experts
    )
    far_tokens = {bits: shift(own, "exp", bits) for bits in range(2, exp_count, 2)}
    partner = shift(own, "exp", 1)
    far_pairs = {bits: [value, shift(value, "exp", 1)] for bits, value in far_tokens.items()}
    total = layer([own], out_type=F32)[0]
    for bits, pair in far_pairs.items():
        mine, theirs = layer(pair, out_type=BF16)
        both = mine.astype(F32) + shift(theirs, "exp", 1).astype(F32)
        total = total + shift(both.astype(BF16), "exp", bits).astype(F32)
    total = total + shift(layer([partner], out_type=BF16)[0], "exp", 1).astype(F32)
    return total.astype(BF16)


def far_expert_layer(moe_input, moe_grad, routes, gates, w_gate, w_up, w_down):
    tok_rows, width_part = moe_input.shape
    fanout = routes.shape[1]
    local_experts = w_gate.shape[0]
    exp_count = lax.axis_size("exp")
    experts = local_experts * exp_count
    capacity = tok_rows * fanout // experts * 5 // 4
    flat_routes = routes.reshape(-1)
    onehot = (flat_routes[:, None] == jnp.arange(experts, dtype=jnp.int32)[None, :]).astype(
        jnp.int32
    )
    before = jnp.cumsum(onehot, axis=0) - onehot
    slot_index = jnp.sum(before * onehot, axis=1)
    target = flat_routes * capacity + slot_index
    source_rows = jnp.arange(tok_rows * fanout, dtype=jnp.int32) // fanout
    empty = jnp.zeros((experts * capacity, width_part), BF16)
    send_shape = (exp_count, local_experts * capacity, width_part)
    send_input = empty.at[target].set(moe_input[source_rows]).reshape(send_shape)
    send_grad = empty.at[target].set(moe_grad[source_rows]).reshape(send_shape)
    recv_input, recv_grad = (
        lax.all_to_all(send_input, "exp", split_axis=0, concat_axis=0, tiled=True),
        lax.all_to_all(send_grad, "exp", split_axis=0, concat_axis=0, tiled=True),
    )
    slot_shape = (exp_count, local_experts, capacity, width_part)
    recv_input = recv_input.reshape(slot_shape)
    recv_grad = recv_grad.reshape(slot_shape)
    gate_part = jnp.einsum("sekd,edh->sekh", recv_input, w_gate, preferred_element_type=F32)
    up_part = jnp.einsum("sekd,edh->sekh", recv_input, w_up, preferred_element_type=F32)
    down_part = jnp.einsum("sekd,ehd->sekh", recv_grad, w_down, preferred_element_type=F32)
    gate_pre, up_pre, hidden_grad = (
        lax.psum(gate_part.astype(BF16), "ctx").astype(F32),
        lax.psum(up_part.astype(BF16), "ctx").astype(F32),
        lax.psum(down_part.astype(BF16), "ctx").astype(F32),
    )
    gate_back, up_back = swiglu_back(gate_pre, up_pre, hidden_grad)
    route_part = jnp.einsum("sekh,edh->sekd", gate_back, w_gate, preferred_element_type=F32)
    route_part = route_part + jnp.einsum(
        "sekh,edh->sekd", up_back, w_up, preferred_element_type=F32
    )
    route_part = route_part.astype(BF16).reshape(send_shape)
    returned = lax.all_to_all(route_part, "exp", split_axis=0, concat_axis=0, tiled=True).reshape(
        experts * capacity, width_part
    )
    per_route = returned[target].reshape(tok_rows, fanout, width_part).astype(F32)
    return jnp.sum(per_route * gates[:, :, None], axis=1).astype(BF16)


def gather_latents(latents):
    across = shift(latents, "ctx", 1)
    along = shift(latents, "ctx", 2)
    return jnp.concatenate([latents, across, along, shift(along, "ctx", 1)], axis=0)


def sum_latent_grad(part):
    shards, keys, width = part.shape
    exp_count = lax.axis_size("exp")
    if exp_count > 8:
        ctx = lax.axis_index("ctx")
        order = jnp.arange(shards) ^ ctx
        whole = part[order].reshape(shards * keys, width)
        return lax.psum_scatter(whole, ("ctx", "exp"), scatter_dimension=0, tiled=True)
    me = lax.axis_index("exp")
    core, chip = me % 2, me // 2
    part = part.reshape(shards, exp_count // 2, 2, keys // exp_count, width)
    keep = lax.dynamic_index_in_dim(part, core, axis=2, keepdims=False)
    give = lax.dynamic_index_in_dim(part, 1 - core, axis=2, keepdims=False).astype(BF16)
    part = keep + shift(give, "exp", 1).astype(F32)
    total = lax.dynamic_index_in_dim(part, chip, axis=1, keepdims=False)
    for bits in range(1, exp_count // 2):
        give = lax.dynamic_index_in_dim(part, chip ^ bits, axis=1, keepdims=False).astype(BF16)
        total = total + shift(give, "exp", 2 * bits).astype(F32)
    out = total[0]
    for bits in range(1, shards):
        out = out + shift(total[bits].astype(BF16), "ctx", bits).astype(F32)
    return out


def attention_layer(queries, out_grad, positions, latents):
    q_rows = queries.shape[0]
    keys, lat_width = latents.shape
    shards = lax.axis_size("ctx")
    head_count = queries.shape[1] // lat_width
    val_width = out_grad.shape[1] // head_count
    query_heads = queries.reshape(q_rows, head_count, lat_width)
    grad_heads = out_grad.reshape(q_rows, head_count, val_width)
    gathered = gather_latents(latents)
    shard_of = jnp.arange(shards, dtype=jnp.int32) ^ lax.axis_index("ctx")
    key_ids = (shard_of[:, None] * keys + jnp.arange(keys, dtype=jnp.int32)[None, :]).reshape(-1)
    visible = (key_ids[None, :] <= positions[:, None])[None]
    scores = (
        jnp.einsum("qhc,kc->hqk", query_heads, gathered, preferred_element_type=F32) * SCORE_SCALE
    )
    scores = jnp.where(visible, scores, MASKED)
    peak = jnp.max(scores, axis=2, keepdims=True)
    raw = jnp.where(visible, jnp.exp(scores - peak), 0.0)
    attend = raw / jnp.sum(raw, axis=2, keepdims=True)
    value_dot = jnp.einsum(
        "qhv,kv->hqk", grad_heads, gathered[:, :val_width], preferred_element_type=F32
    )
    row_dot = jnp.sum(attend * value_dot, axis=2, keepdims=True)
    score_grad = (attend * (value_dot - row_dot)).astype(BF16)
    query_grad = (
        jnp.einsum("hqk,kc->qhc", score_grad, gathered, preferred_element_type=F32) * SCORE_SCALE
    )
    key_grad = (
        jnp.einsum("hqk,qhc->kc", score_grad, query_heads, preferred_element_type=F32)
        * SCORE_SCALE
    )
    value_grad = jnp.einsum(
        "hqk,qhv->kv", attend.astype(BF16), grad_heads, preferred_element_type=F32
    )
    latent_part = key_grad + jnp.pad(value_grad, ((0, 0), (0, lat_width - val_width)))
    latent_grad = sum_latent_grad(latent_part.reshape(shards, keys, lat_width))
    query_out = query_grad.astype(BF16).reshape(q_rows, head_count * lat_width)
    return (query_out, latent_grad)


def per_device(
    moe_input, moe_grad, routes, gates, w_gate, w_up, w_down, queries, out_grad, positions, latents
):
    near = lax.axis_size("exp") <= routes.shape[1]
    expert_layer = near_expert_layer if near else far_expert_layer
    query_out, latent_grad = attention_layer(queries, out_grad, positions, latents)
    input_grad = expert_layer(moe_input, moe_grad, routes, gates, w_gate, w_up, w_down)
    return (input_grad, query_out, latent_grad)


def solution(mesh):
    return jax.shard_map(
        per_device,
        mesh=mesh,
        in_specs=(
            P("exp", "ctx"),
            P("exp", "ctx"),
            P("exp", None),
            P("exp", None),
            P("exp", "ctx", None),
            P("exp", "ctx", None),
            P("exp", None, "ctx"),
            P("ctx", "exp"),
            P("ctx", "exp"),
            P("ctx"),
            P("ctx", None),
        ),
        out_specs=(P("exp", "ctx"), P("ctx", "exp"), P(("ctx", "exp"), None)),
        check_vma=False,
    )
```

```python
import functools

import jax
import jax.numpy as jnp
from jax import lax
from jax.experimental import pallas as pl
from jax.experimental.pallas import tpu as pltpu
from jax.sharding import PartitionSpec as P

SCORE_SCALE = 192.0 ** (-0.5)
MASKED = -1e30
BF16 = jnp.bfloat16
F32 = jnp.float32
META = 128
VMEM_LIMIT = 16 * 1024 * 1024
AHEAD = 3
FIRST_VMEM_LIMIT = 40 * 10**6


def swiglu_back(gate_pre, up_pre, hidden_grad):
    sigma = jax.nn.sigmoid(gate_pre)
    gate_back = hidden_grad * up_pre * sigma * (1.0 + gate_pre * (1.0 - sigma))
    up_back = hidden_grad * gate_pre * sigma
    return (gate_back.astype(BF16), up_back.astype(BF16))


def shift(value, bits, name):
    pairs = [(i, i ^ bits) for i in range(lax.axis_size("exp"))]
    with jax.named_scope(name):
        return lax.ppermute(value, "exp", pairs)


def declared(length):
    return pl.CostEstimate(
        flops=int(length * 10**9) + 1, bytes_accessed=int(length * 3 * 10**6) + 1, transcendentals=0
    )


LENGTH = [1]


def call(kernel, args, in_specs, out_shape, out_specs, deps=(), grid=(), scratch=(), limit=None, name=None):
    count = len(args)

    def body(*refs):
        kernel(*refs[:count], *refs[count + len(deps) :])

    return pl.pallas_call(
        body,
        out_shape=out_shape,
        grid=grid,
        in_specs=list(in_specs) + [pl.BlockSpec(memory_space=pl.ANY)] * len(deps),
        out_specs=out_specs,
        scratch_shapes=scratch,
        compiler_params=pltpu.CompilerParams(vmem_limit_bytes=limit or VMEM_LIMIT),
        cost_estimate=declared(LENGTH[0]),
        name=name,
    )(*args, *deps)


def dot(left, right):
    return jnp.dot(left, right, preferred_element_type=F32)


def dot_t(left, right):
    return lax.dot_general(left, right, (((1,), (1,)), ((), ())), preferred_element_type=F32)


def pack(experts, routes, gates, rows_in, rows_grad, out_ref):
    rows, width = rows_in.shape
    out_ref[:, :width] = rows_in
    out_ref[:, width : 2 * width] = rows_grad
    lane = lax.broadcasted_iota(jnp.int32, (rows, META), 1)
    expert = lane % experts
    section = lane // experts
    gate = jnp.zeros((rows, META), F32)
    named = jnp.zeros((rows, META), F32)
    for k in range(routes.shape[1]):
        hit = routes[:, k : k + 1] == expert
        gate = gate + jnp.where(hit, gates[:, k : k + 1], 0.0)
        named = named + jnp.where(hit, 1.0, 0.0)
    low = lax.broadcasted_iota(jnp.int32, (rows, rows), 0)
    high = lax.broadcasted_iota(jnp.int32, (rows, rows), 1)
    before = jnp.where(high < low, 1.0, 0.0).astype(BF16)
    slot = jnp.where(named > 0.0, dot(before, named.astype(BF16)), -1.0)
    gate_high = gate.astype(BF16).astype(F32)
    meta = jnp.where(section == 0, gate_high, jnp.where(section == 1, gate - gate_high, slot))
    out_ref[:, 2 * width :] = meta.astype(BF16)


def pack_kernel(experts, routes_ref, gates_ref, input_ref, grad_ref, out_ref):
    pack(experts, routes_ref[...].T, gates_ref[...].T, input_ref[...], grad_ref[...], out_ref)


def pack_tokens(moe_input, moe_grad, routes, gates, experts):
    rows, width = moe_input.shape
    return call(
        functools.partial(pack_kernel, experts),
        [routes.T, gates.T, moe_input, moe_grad],
        in_vmem(4),
        jax.ShapeDtypeStruct((rows, 2 * width + META), BF16),
        in_vmem(1)[0],
        name="pack_tokens",
    )


def first_kernel(blocks, experts, capacity, plan_ref, *refs):
    token_refs, args, refs = refs[:blocks], refs[blocks : blocks + 3], refs[blocks + 3 :]
    send_ref, keep_ref = refs[:2]
    weights, sem = refs[2:5], refs[5]
    local = weights[0].shape[0]
    quarter = weights[0].shape[2] // 4
    copies = [
        pltpu.make_async_copy(args[m].at[e], weights[m].at[e], sem.at[3 * e + m])
        for e in range(local)
        for m in range(3)
    ]
    for copy in copies[:AHEAD]:
        copy.start()
    for e in range(local):
        rows = slot_rows(plan_ref, e, experts, capacity, token_refs)
        for m in range(3):
            copies[3 * e + m].wait()
            if 3 * e + m + AHEAD < len(copies):
                copies[3 * e + m + AHEAD].start()
            for place, out_ref in ((1, send_ref), (3, keep_ref)):
                for j in range(2):
                    part = columns(plan_ref, place + j, quarter)
                    if m < 2:
                        value = dot(rows[0], weights[m][e, :, part])
                    else:
                        value = dot_t(rows[1], weights[m][e, part, :])
                    out_ref[j, e, m] = value.astype(BF16)


def first_products(plan, tokens, weights, capacity, experts):
    local, _, hidden = weights[0].shape
    part = jax.ShapeDtypeStruct((2, local, 3, len(tokens) * capacity, hidden // 4), BF16)
    return call(
        functools.partial(first_kernel, len(tokens), experts, capacity),
        [plan, *tokens, *weights],
        [pl.BlockSpec(memory_space=pltpu.SMEM)]
        + in_vmem(len(tokens))
        + [pl.BlockSpec(memory_space=pltpu.HBM)] * 3,
        [part, part] + [jax.ShapeDtypeStruct(w.shape, w.dtype) for w in weights],
        in_vmem(5),
        scratch=[pltpu.SemaphoreType.DMA((3 * local,))],
        limit=FIRST_VMEM_LIMIT,
        name="first_products",
    )


def slot_rows(plan_ref, expert, experts, capacity, token_refs):
    width = (token_refs[0].shape[1] - META) // 2
    tokens = token_refs[0].shape[0]
    lane = lax.broadcasted_iota(jnp.int32, (16, META), 1)
    pick = jnp.where(lane == 2 * experts + plan_ref[0] + expert, 1.0, 0.0).astype(BF16)
    slot = lax.broadcasted_iota(jnp.int32, (capacity, tokens), 0)
    parts_in, parts_grad = [], []
    for token_ref in token_refs:
        slot_of = dot_t(pick, token_ref[:, 2 * width :])[0:1, :].astype(jnp.int32)
        chosen = jnp.where(slot == slot_of, 1.0, 0.0).astype(BF16)
        parts_in.append(dot(chosen, token_ref[:, :width]).astype(BF16))
        parts_grad.append(dot(chosen, token_ref[:, width : 2 * width]).astype(BF16))
    return jnp.concatenate(parts_in, axis=0), jnp.concatenate(parts_grad, axis=0)


def columns(plan_ref, place, quarter):
    return pl.ds(pl.multiple_of(plan_ref[place] * quarter, quarter), quarter)


def products_kernel(blocks, experts, capacity, plan_ref, *refs):
    token_refs = refs[:blocks]
    gate_ref, up_ref, down_ref, send_ref, keep_ref = refs[blocks:]
    local = gate_ref.shape[0]
    quarter = gate_ref.shape[2] // 4
    rows = [slot_rows(plan_ref, e, experts, capacity, token_refs) for e in range(local)]
    for place, out_ref in ((1, send_ref), (3, keep_ref)):
        for j in range(2):
            part = columns(plan_ref, place + j, quarter)
            for e in range(local):
                out_ref[j, e, 0] = dot(rows[e][0], gate_ref[e, :, part]).astype(BF16)
                out_ref[j, e, 1] = dot(rows[e][0], up_ref[e, :, part]).astype(BF16)
                out_ref[j, e, 2] = dot_t(rows[e][1], down_ref[e, part, :]).astype(BF16)


def in_vmem(count):
    return [pl.BlockSpec(memory_space=pltpu.VMEM)] * count


def products(plan, tokens, w_gate, w_up, w_down, capacity, experts, deps):
    local, _, hidden = w_gate.shape
    slots = len(tokens) * capacity
    shape = jax.ShapeDtypeStruct((2, local, 3, slots, hidden // 4), BF16)
    return call(
        functools.partial(products_kernel, len(tokens), experts, capacity),
        [plan, *tokens, w_gate, w_up, w_down],
        [pl.BlockSpec(memory_space=pltpu.SMEM)] + in_vmem(len(tokens) + 3),
        [shape, shape],
        in_vmem(2),
        deps,
        name="products",
    )


def add_kernel(*refs):
    *terms, out_ref = refs
    value = terms[0][...].astype(F32)
    for term in terms[1:]:
        value = value + term[...].astype(F32)
    out_ref[...] = value.astype(out_ref.dtype)


def part_spec(part, shape):
    zeros = (0,) * (len(shape) - 1)
    return pl.BlockSpec((None, *shape[1:]), lambda i: (part, *zeros))


def add_parts(terms, dtype, deps=()):
    shape = terms[0][0].shape[1:]
    return call(
        add_kernel,
        [term for term, _ in terms],
        [part_spec(part, term.shape) for term, part in terms],
        jax.ShapeDtypeStruct(shape, dtype),
        pl.BlockSpec(shape, lambda i: (0,) * len(shape)),
        deps,
        grid=(1,),
        name="add_parts",
    )


def back_kernel(got_ref, kept_ref, other_ref, out_ref):
    for e in range(out_ref.shape[0]):
        gate_pre, up_pre, hidden_grad = (
            got_ref[0, e, m].astype(F32) + kept_ref[0, e, m].astype(F32) + other_ref[e, m].astype(F32)
            for m in range(3)
        )
        out_ref[e, 0], out_ref[e, 1] = swiglu_back(gate_pre, up_pre, hidden_grad)


def hidden_back(got, kept, other, deps):
    _, local, _, slots, quarter = got.shape
    last = pl.BlockSpec((1, local, 3, slots, quarter), lambda i: (1, 0, 0, 0, 0))
    return call(
        back_kernel,
        [got, kept, other],
        [last, last, pl.BlockSpec((local, 3, slots, quarter), lambda i: (0, 0, 0, 0))],
        jax.ShapeDtypeStruct((local, 2, slots, quarter), BF16),
        pl.BlockSpec((local, 2, slots, quarter), lambda i: (0, 0, 0, 0)),
        deps,
        grid=(1,),
        name="hidden_back",
    )


def join_kernel(own_ref, other_ref, out_ref):
    out_ref[0] = own_ref[...]
    out_ref[1] = other_ref[...]


def join(own, other, deps):
    shape = jax.ShapeDtypeStruct((2, *own.shape), own.dtype)
    return call(join_kernel, [own, other], in_vmem(2), shape, in_vmem(1)[0], deps, name="join")


def route_kernel(blocks, mine, experts, capacity, plan_ref, *refs):
    meta_refs, refs = refs[:blocks], refs[blocks:]
    piece_refs, (gate_ref, up_ref), out_refs = refs[:2], refs[2:4], refs[4:]
    local = gate_ref.shape[0]
    quarter = gate_ref.shape[2] // 4
    tokens = meta_refs[0].shape[0]
    row = lax.broadcasted_iota(jnp.int32, (META, META), 0)
    lane = lax.broadcasted_iota(jnp.int32, (META, META), 1)
    slot = lax.broadcasted_iota(jnp.int32, (tokens, capacity), 1)
    totals = [None] * blocks
    for e in range(local):
        route = None
        for p in range(4):
            piece_ref = piece_refs[p // 2]
            part = columns(plan_ref, 5 + p, quarter)
            value = dot_t(piece_ref[p % 2, e, 0], gate_ref[e, :, part])
            value = value + dot_t(piece_ref[p % 2, e, 1], up_ref[e, :, part])
            route = value if route is None else route + value
        route = route.astype(BF16)
        pick = jnp.where(lane == row * experts + plan_ref[0] + e, 1.0, 0.0).astype(BF16)
        for b in range(blocks):
            found = dot_t(meta_refs[b][...], pick)
            named = found[:, 2:3].astype(jnp.int32) == slot
            high = jnp.where(named, found[:, 0:1], 0.0).astype(BF16)
            low = jnp.where(named, found[:, 1:2], 0.0).astype(BF16)
            own = route[b * capacity : (b + 1) * capacity, :]
            value = dot(high, own) + dot(low, own)
            totals[b] = value if totals[b] is None else totals[b] + value
    out_refs = list(out_refs)
    if mine:
        mine_ref = out_refs.pop(0)
        for b in range(mine):
            mine_ref[b] = totals[b]
    for b in range(mine, blocks):
        out_refs[0][b - mine] = totals[b].astype(BF16)


def route_sums(plan, tokens, mine, pieces, w_gate, w_up, capacity, experts, deps):
    width = w_gate.shape[1]
    blocks = len(tokens)
    count = tokens[0].shape[0]
    meta_at = 2 * width // META
    out_shape = []
    if mine:
        out_shape.append(jax.ShapeDtypeStruct((mine, count, width), F32))
    if blocks > mine:
        out_shape.append(jax.ShapeDtypeStruct((blocks - mine, count, width), BF16))
    return call(
        functools.partial(route_kernel, blocks, mine, experts, capacity),
        [plan, *tokens, *pieces, w_gate, w_up],
        [pl.BlockSpec(memory_space=pltpu.SMEM)]
        + [pl.BlockSpec((count, META), lambda i: (0, meta_at))] * blocks
        + in_vmem(4),
        out_shape,
        in_vmem(len(out_shape)),
        deps,
        grid=(1,),
        name="route_sums",
    )


def plane_shift(value, near, name):
    count = lax.axis_size("exp")
    pairs = []
    for c in range(lax.axis_size("ctx")):
        for i in range(count):
            bits = 1 if (i % 2 == 0) == near else 2
            pairs.append((c * count + i, (c ^ bits) * count + i))
    with jax.named_scope(name):
        return lax.ppermute(value, ("ctx", "exp"), pairs)


class Chunk:
    def __init__(self, name, plan, weights, capacity, experts, mine):
        self.name, self.plan, self.weights, self.mine = name, plan, weights, mine
        self.capacity, self.experts = capacity, experts

    def multiply(self, tokens, *deps):
        return self.begin(
            tokens, *products(self.plan, tokens, *self.weights, self.capacity, self.experts, deps)
        )

    def begin(self, tokens, send, kept):
        self.tokens, self.kept = tokens, kept
        self.got = plane_shift(send, True, self.name + "_sums_near")
        return kept

    def add(self, *deps):
        half = add_parts([(self.got, 0), (self.kept, 0)], BF16, deps)
        self.other = plane_shift(half, False, self.name + "_sums_far")
        return half

    def turn(self, *deps):
        self.own = hidden_back(self.got, self.kept, self.other, deps)
        self.from_far = plane_shift(self.own, False, self.name + "_own_far")
        return self.own

    def forward(self, *deps):
        self.joined = join(self.own, self.from_far, deps)
        self.from_near = plane_shift(self.joined, True, self.name + "_both_near")
        return self.joined

    def finish(self, *deps):
        return route_sums(
            self.plan,
            self.tokens,
            self.mine,
            [self.joined, self.from_near],
            *self.weights[:2],
            self.capacity,
            self.experts,
            deps,
        )


def near_layers(
    moe_input, moe_grad, routes, gates, w_gate, w_up, w_down, queries, out_grad, positions, latents
):
    tok_rows = moe_input.shape[0]
    fanout = routes.shape[1]
    local = w_gate.shape[0]
    exp_count = lax.axis_size("exp")
    experts = local * exp_count
    capacity = tok_rows * fanout // experts * 5 // 4
    ctx, exp = lax.axis_index("ctx"), lax.axis_index("exp")
    x, y = ctx % 2, ctx // 2
    near = jnp.where(exp % 2 == 0, x, y)
    far = jnp.where(exp % 2 == 0, y, x)
    near_bit = jnp.where(exp % 2 == 0, 1, 2)
    plan = jnp.stack(
        [
            exp * local,
            (1 - near) * 2 + 1 - far,
            (1 - near) * 2 + far,
            near * 2 + 1 - far,
            near * 2 + far,
            near * 2 + far,
            near * 2 + 1 - far,
            (1 - near) * 2 + far,
            (1 - near) * 2 + 1 - far,
            exp,
            ctx,
            ctx ^ (3 - near_bit),
            ctx ^ near_bit,
            ctx ^ 3,
        ]
    ).astype(jnp.int32)

    def chunk(name, mine):
        return Chunk(name, plan, weights, capacity, experts, mine)

    own = pack_tokens(moe_input, moe_grad, routes, gates, experts)
    partner = shift(own, 1, "partner_move")
    first = [own, partner]
    LENGTH[0] = 10
    send, kept, *weights = first_products(plan, first, (w_gate, w_up, w_down), capacity, experts)
    a = chunk("a", 1)
    from_1 = shift(own, 2, "from_1_move")
    from_3 = shift(own, 6, "from_3_move")
    other_1 = shift(from_1, 1, "other_1_move")
    other_3 = shift(from_3, 1, "other_3_move")
    from_2 = shift(from_3, 2, "from_2_move")
    other_2 = shift(from_2, 1, "other_2_move")
    keys = latents.T
    keys_near = plane_shift(keys, True, "keys_near_move")
    keys_far = plane_shift(keys, False, "keys_far_move")
    keys_both = plane_shift(keys_near, False, "keys_both_move")
    made = {}

    def attend(*deps):
        made["queries"], give, made["keep"] = attention(
            plan, queries, out_grad, positions, [keys, keys_far, keys_near, keys_both], deps
        )
        made["got"] = shift(give, 1, "got_move")
        return made["keep"]

    def latent_cores(*deps):
        made["cores"] = both = add_parts([(made["keep"][None], 0), (made["got"][None], 0)], BF16, deps)
        made["terms"] = [shift(both[i], 2 * i, "latent_terms") for i in range(1, exp_count // 2)]
        return both

    def latent_chips(*deps):
        terms = [(made["cores"], 0)] + [(term[None], 0) for term in made["terms"]]
        made["chips"] = both = add_parts(terms, BF16, deps)
        made["crossed"] = plane_shift(both[2:], True, "crossed_move")
        return both

    def latent_near(*deps):
        terms = [(made["chips"][None, :2], 0), (made["crossed"][None], 0)]
        made["pair"] = both = add_parts(terms, BF16, deps)
        made["last"] = plane_shift(both[1], False, "last_move")
        return both

    def latent_far(*deps):
        terms = [(made["pair"], 0), (made["last"][None], 0)]
        made["latents"] = add_parts(terms, F32, deps)
        return made["latents"]

    def start_total(*deps):
        made["total"], theirs = a.finish(*deps)
        made["more"] = [(shift(theirs, 1, "a_other_move"), 0)]
        return theirs

    def finish(chunk):
        def act(*deps):
            *mine, theirs = chunk.finish(*deps)
            made[chunk.name] = mine
            made[chunk.name + "_other"] = shift(theirs, 1, chunk.name + "_other_move")
            return theirs

        return act

    def send_back(chunk, bits):
        def act(*deps):
            made[chunk.name + "_back"] = []
            for place, bit in enumerate(bits):
                terms = [(made[chunk.name][0], place), (made[chunk.name + "_other"], place)]
                both = add_parts(terms, BF16, deps)
                back = shift(both, bit, chunk.name + "_back_move")
                made[chunk.name + "_back"].append((back[None], 0))
            return both

        return act

    def receive(chunk, last):
        def act(*deps):
            terms = [(made["total"], 0)] + made.pop("more", []) + made[chunk.name + "_back"]
            total = add_parts(terms, BF16 if last else F32, deps)
            made["total"] = total[None]
            return total

        return act

    b = chunk("b", 1)
    c = chunk("c", 1)
    d = chunk("d", 1)
    order = (
        (a.add, 2),
        (a.turn, 2),
        (functools.partial(b.multiply, [from_1, other_1]), 2),
        (attend, 2),
        (a.forward, 2),
        (b.add, 2),
        (start_total, 2),
        (functools.partial(c.multiply, [from_3, other_3]), 2),
        (b.turn, 2),
        (latent_cores, 2),
        (b.forward, 2),
        (c.add, 2),
        (functools.partial(d.multiply, [from_2, other_2]), 2),
        (finish(b), 2),
        (latent_chips, 2),
        (c.turn, 2),
        (send_back(b, (2,)), 2),
        (d.add, 2),
        (c.forward, 2),
        (latent_near, 2),
        (d.turn, 2),
        (finish(c), 2),
        (receive(b, False), 2),
        (d.forward, 2),
        (send_back(c, (6,)), 2),
        (latent_far, 2),
        (receive(c, False), 2),
        (finish(d), 2),
        (send_back(d, (4,)), 2),
        (receive(d, True), 2),
    )
    step = a.begin(first, send, kept)
    for act, length, *waits in order:
        LENGTH[0] = length
        step = act(step, *waits)
    return (made["total"][0], made["queries"], made["latents"])


def attention_kernel(heads, plan_ref, queries_ref, grads_ref, positions_ref, *refs):
    key_refs, (query_ref, give_ref, keep_ref, total_ref) = refs[:4], refs[4:]
    rows = queries_ref.shape[0]
    width, keys = key_refs[0].shape
    values = grads_ref.shape[1] // heads
    chips, shards, own_keys, _ = give_ref.shape
    square = lax.broadcasted_iota(jnp.int32, (rows, rows), 0)
    diagonal = square == lax.broadcasted_iota(jnp.int32, (rows, rows), 1)
    position = jnp.sum(
        jnp.where(diagonal, positions_ref[...].astype(F32), 0.0), axis=1, keepdims=True
    ).astype(jnp.int32)
    offset = lax.broadcasted_iota(jnp.int32, (rows, keys), 1)
    visible = [offset + plan_ref[10 + r] * keys <= position for r in range(shards)]
    outs = []
    for h in range(heads):
        query = queries_ref[:, h * width : (h + 1) * width]
        grad = grads_ref[:, h * values : (h + 1) * values]
        scores = [
            jnp.where(visible[r], dot(query, key_refs[r][...]) * SCORE_SCALE, MASKED)
            for r in range(shards)
        ]
        peak = functools.reduce(jnp.maximum, scores)
        peak = jnp.max(peak, axis=1, keepdims=True)
        raw = [jnp.where(visible[r], jnp.exp(scores[r] - peak), 0.0) for r in range(shards)]
        whole = jnp.sum(functools.reduce(jnp.add, raw), axis=1, keepdims=True)
        attend = [part / whole for part in raw]
        value_dot = [dot(grad, key_refs[r][:values, :]) for r in range(shards)]
        row_dot = functools.reduce(jnp.add, [a * v for a, v in zip(attend, value_dot)])
        row_dot = jnp.sum(row_dot, axis=1, keepdims=True)
        query_grad = None
        for r in range(shards):
            score_grad = (attend[r] * (value_dot[r] - row_dot)).astype(BF16)
            term = dot_t(score_grad, key_refs[r][...])
            query_grad = term if query_grad is None else query_grad + term
            key_grad = dot_rows(score_grad, query) * SCORE_SCALE
            value_grad = dot_rows(attend[r].astype(BF16), grad)
            part = pl.ds(r * keys, keys)
            if h == 0:
                total_ref[part, :] = key_grad
            else:
                total_ref[part, :] += key_grad
            total_ref[part, :values] += value_grad
        outs.append((query_grad * SCORE_SCALE).astype(BF16))
    query_ref[...] = jnp.concatenate(outs, axis=1)
    core, chip = plan_ref[9] % 2, plan_ref[9] // 2
    for b in range(chips):
        for r in range(shards):
            start = r * keys + (chip ^ b) * (2 * own_keys)
            across = (r % 2) * 2 + r // 2
            for out_ref, which, place in ((give_ref, 1 - core, across), (keep_ref, core, r)):
                at = pl.multiple_of(start + which * own_keys, own_keys)
                out_ref[b, place] = total_ref[pl.ds(at, own_keys), :].astype(BF16)


def dot_rows(left, right):
    return lax.dot_general(left, right, (((0,), (0,)), ((), ())), preferred_element_type=F32)


def attention(plan, queries, out_grad, positions, keys, deps):
    rows = queries.shape[0]
    width, count = keys[0].shape
    heads = queries.shape[1] // width
    exp_count = lax.axis_size("exp")
    terms = jax.ShapeDtypeStruct((exp_count // 2, len(keys), count // exp_count, width), BF16)
    return call(
        functools.partial(attention_kernel, heads),
        [plan, queries, out_grad, positions.reshape(1, rows), *keys],
        [pl.BlockSpec(memory_space=pltpu.SMEM)] + in_vmem(3 + len(keys)),
        [jax.ShapeDtypeStruct(queries.shape, BF16), terms, terms],
        in_vmem(3),
        deps,
        scratch=[pltpu.VMEM((len(keys) * count, width), F32)],
        name="attention",
    )


def far_expert_layer(moe_input, moe_grad, routes, gates, w_gate, w_up, w_down):
    tok_rows, width_part = moe_input.shape
    fanout = routes.shape[1]
    local_experts = w_gate.shape[0]
    exp_count = lax.axis_size("exp")
    experts = local_experts * exp_count
    capacity = tok_rows * fanout // experts * 5 // 4
    flat_routes = routes.reshape(-1)
    onehot = (flat_routes[:, None] == jnp.arange(experts, dtype=jnp.int32)[None, :]).astype(
        jnp.int32
    )
    before = jnp.cumsum(onehot, axis=0) - onehot
    slot_index = jnp.sum(before * onehot, axis=1)
    target = flat_routes * capacity + slot_index
    source_rows = jnp.arange(tok_rows * fanout, dtype=jnp.int32) // fanout
    empty = jnp.zeros((experts * capacity, width_part), BF16)
    send_shape = (exp_count, local_experts * capacity, width_part)
    send_input = empty.at[target].set(moe_input[source_rows]).reshape(send_shape)
    send_grad = empty.at[target].set(moe_grad[source_rows]).reshape(send_shape)
    recv_input, recv_grad = (
        lax.all_to_all(send_input, "exp", split_axis=0, concat_axis=0, tiled=True),
        lax.all_to_all(send_grad, "exp", split_axis=0, concat_axis=0, tiled=True),
    )
    slot_shape = (exp_count, local_experts, capacity, width_part)
    recv_input = recv_input.reshape(slot_shape)
    recv_grad = recv_grad.reshape(slot_shape)
    gate_part = jnp.einsum("sekd,edh->sekh", recv_input, w_gate, preferred_element_type=F32)
    up_part = jnp.einsum("sekd,edh->sekh", recv_input, w_up, preferred_element_type=F32)
    down_part = jnp.einsum("sekd,ehd->sekh", recv_grad, w_down, preferred_element_type=F32)
    gate_pre, up_pre, hidden_grad = (
        lax.psum(gate_part.astype(BF16), "ctx").astype(F32),
        lax.psum(up_part.astype(BF16), "ctx").astype(F32),
        lax.psum(down_part.astype(BF16), "ctx").astype(F32),
    )
    gate_back, up_back = swiglu_back(gate_pre, up_pre, hidden_grad)
    route_part = jnp.einsum("sekh,edh->sekd", gate_back, w_gate, preferred_element_type=F32)
    route_part = route_part + jnp.einsum(
        "sekh,edh->sekd", up_back, w_up, preferred_element_type=F32
    )
    route_part = route_part.astype(BF16).reshape(send_shape)
    returned = lax.all_to_all(route_part, "exp", split_axis=0, concat_axis=0, tiled=True).reshape(
        experts * capacity, width_part
    )
    per_route = returned[target].reshape(tok_rows, fanout, width_part).astype(F32)
    return jnp.sum(per_route * gates[:, :, None], axis=1).astype(BF16)


def sum_latent_grad(part):
    keys, width = part.shape
    shards, exp_count = lax.axis_size("ctx"), lax.axis_size("exp")
    part = part.reshape(shards, exp_count, keys // shards // exp_count, width).swapaxes(0, 1)
    part = part.reshape(keys, width).astype(BF16)
    part = lax.psum_scatter(part, "exp", scatter_dimension=0, tiled=True)
    return lax.psum_scatter(part.astype(F32), "ctx", scatter_dimension=0, tiled=True)


def attention_layer(queries, out_grad, positions, latents):
    q_rows = queries.shape[0]
    lat_width = latents.shape[1]
    head_count = queries.shape[1] // lat_width
    val_width = out_grad.shape[1] // head_count
    query_heads = queries.reshape(q_rows, head_count, lat_width)
    grad_heads = out_grad.reshape(q_rows, head_count, val_width)
    gathered = lax.all_gather(latents, "ctx", axis=0, tiled=True)
    key_ids = jnp.arange(gathered.shape[0], dtype=jnp.int32)
    visible = (key_ids[None, :] <= positions[:, None])[None]
    scores = (
        jnp.einsum("qhc,kc->hqk", query_heads, gathered, preferred_element_type=F32) * SCORE_SCALE
    )
    scores = jnp.where(visible, scores, MASKED)
    peak = jnp.max(scores, axis=2, keepdims=True)
    raw = jnp.where(visible, jnp.exp(scores - peak), 0.0)
    attend = raw / jnp.sum(raw, axis=2, keepdims=True)
    value_dot = jnp.einsum(
        "qhv,kv->hqk", grad_heads, gathered[:, :val_width], preferred_element_type=F32
    )
    row_dot = jnp.sum(attend * value_dot, axis=2, keepdims=True)
    score_grad = (attend * (value_dot - row_dot)).astype(BF16)
    query_grad = (
        jnp.einsum("hqk,kc->qhc", score_grad, gathered, preferred_element_type=F32) * SCORE_SCALE
    )
    key_grad = (
        jnp.einsum("hqk,qhc->kc", score_grad, query_heads, preferred_element_type=F32)
        * SCORE_SCALE
    )
    value_grad = jnp.einsum(
        "hqk,qhv->kv", attend.astype(BF16), grad_heads, preferred_element_type=F32
    )
    latent_part = key_grad + jnp.pad(value_grad, ((0, 0), (0, lat_width - val_width)))
    latent_grad = sum_latent_grad(latent_part)
    query_out = query_grad.astype(BF16).reshape(q_rows, head_count * lat_width)
    return (query_out, latent_grad)


def per_device(
    moe_input, moe_grad, routes, gates, w_gate, w_up, w_down, queries, out_grad, positions, latents
):
    if lax.axis_size("exp") <= routes.shape[1]:
        return near_layers(
            moe_input, moe_grad, routes, gates, w_gate, w_up, w_down,
            queries, out_grad, positions, latents,
        )
    query_out, latent_grad = attention_layer(queries, out_grad, positions, latents)
    input_grad = far_expert_layer(moe_input, moe_grad, routes, gates, w_gate, w_up, w_down)
    return (input_grad, query_out, latent_grad)


def solution(mesh):
    return jax.shard_map(
        per_device,
        mesh=mesh,
        in_specs=(
            P("exp", "ctx"),
            P("exp", "ctx"),
            P("exp", None),
            P("exp", None),
            P("exp", "ctx", None),
            P("exp", "ctx", None),
            P("exp", None, "ctx"),
            P("ctx", "exp"),
            P("ctx", "exp"),
            P("ctx"),
            P("ctx", None),
        ),
        out_specs=(P("exp", "ctx"), P("ctx", "exp"), P(("ctx", "exp"), None)),
        check_vma=False,
    )
```

```python
import functools

import jax
import jax.numpy as jnp
from jax import lax
from jax.experimental import pallas as pl
from jax.experimental.pallas import tpu as pltpu
from jax.sharding import PartitionSpec as P

SCORE_SCALE = 192.0 ** (-0.5)
MASKED = -1e30
BF16 = jnp.bfloat16
F32 = jnp.float32
META = 128
VMEM_LIMIT = 16 * 1024 * 1024
AHEAD = 3
FIRST_VMEM_LIMIT = 40 * 10**6


def swiglu_back(gate_pre, up_pre, hidden_grad):
    sigma = jax.nn.sigmoid(gate_pre)
    gate_back = hidden_grad * up_pre * sigma * (1.0 + gate_pre * (1.0 - sigma))
    up_back = hidden_grad * gate_pre * sigma
    return (gate_back.astype(BF16), up_back.astype(BF16))


def shift(value, bits, name):
    pairs = [(i, i ^ bits) for i in range(lax.axis_size("exp"))]
    with jax.named_scope(name):
        return lax.ppermute(value, "exp", pairs)


def declared(length):
    return pl.CostEstimate(
        flops=int(length * 10**9) + 1, bytes_accessed=int(length * 3 * 10**6) + 1, transcendentals=0
    )


LENGTH = [1]


def call(kernel, args, in_specs, out_shape, out_specs, deps=(), grid=(), scratch=(), limit=None, name=None):
    count = len(args)

    def body(*refs):
        kernel(*refs[:count], *refs[count + len(deps) :])

    return pl.pallas_call(
        body,
        out_shape=out_shape,
        grid=grid,
        in_specs=list(in_specs) + [pl.BlockSpec(memory_space=pl.ANY)] * len(deps),
        out_specs=out_specs,
        scratch_shapes=scratch,
        compiler_params=pltpu.CompilerParams(vmem_limit_bytes=limit or VMEM_LIMIT),
        cost_estimate=declared(LENGTH[0]),
        name=name,
    )(*args, *deps)


def dot(left, right):
    return jnp.dot(left, right, preferred_element_type=F32)


def dot_t(left, right):
    return lax.dot_general(left, right, (((1,), (1,)), ((), ())), preferred_element_type=F32)


def pack(experts, routes, gates, rows_in, rows_grad, out_ref):
    rows, width = rows_in.shape
    out_ref[:, :width] = rows_in
    out_ref[:, width : 2 * width] = rows_grad
    lane = lax.broadcasted_iota(jnp.int32, (rows, META), 1)
    expert = lane % experts
    section = lane // experts
    gate = jnp.zeros((rows, META), F32)
    named = jnp.zeros((rows, META), F32)
    for k in range(routes.shape[1]):
        hit = routes[:, k : k + 1] == expert
        gate = gate + jnp.where(hit, gates[:, k : k + 1], 0.0)
        named = named + jnp.where(hit, 1.0, 0.0)
    low = lax.broadcasted_iota(jnp.int32, (rows, rows), 0)
    high = lax.broadcasted_iota(jnp.int32, (rows, rows), 1)
    before = jnp.where(high < low, 1.0, 0.0).astype(BF16)
    slot = jnp.where(named > 0.0, dot(before, named.astype(BF16)), -1.0)
    gate_high = gate.astype(BF16).astype(F32)
    meta = jnp.where(section == 0, gate_high, jnp.where(section == 1, gate - gate_high, slot))
    out_ref[:, 2 * width :] = meta.astype(BF16)


def pack_kernel(experts, routes_ref, gates_ref, input_ref, grad_ref, out_ref):
    pack(experts, routes_ref[...].T, gates_ref[...].T, input_ref[...], grad_ref[...], out_ref)


def pack_tokens(moe_input, moe_grad, routes, gates, experts):
    rows, width = moe_input.shape
    return call(
        functools.partial(pack_kernel, experts),
        [routes.T, gates.T, moe_input, moe_grad],
        in_vmem(4),
        jax.ShapeDtypeStruct((rows, 2 * width + META), BF16),
        in_vmem(1)[0],
        name="pack_tokens",
    )


def first_kernel(blocks, experts, capacity, plan_ref, *refs):
    token_refs, args, refs = refs[:blocks], refs[blocks : blocks + 3], refs[blocks + 3 :]
    send_ref, keep_ref = refs[:2]
    weights, sem = refs[2:5], refs[5]
    local = weights[0].shape[0]
    quarter = weights[0].shape[2] // 4
    copies = [
        pltpu.make_async_copy(args[m].at[e], weights[m].at[e], sem.at[3 * e + m])
        for e in range(local)
        for m in range(3)
    ]
    for copy in copies[:AHEAD]:
        copy.start()
    for e in range(local):
        rows = slot_rows(plan_ref, e, experts, capacity, token_refs)
        for m in range(3):
            copies[3 * e + m].wait()
            if 3 * e + m + AHEAD < len(copies):
                copies[3 * e + m + AHEAD].start()
            for place, out_ref in ((1, send_ref), (3, keep_ref)):
                for j in range(2):
                    part = columns(plan_ref, place + j, quarter)
                    if m < 2:
                        value = dot(rows[0], weights[m][e, :, part])
                    else:
                        value = dot_t(rows[1], weights[m][e, part, :])
                    out_ref[j, e, m] = value.astype(BF16)


def first_products(plan, tokens, weights, capacity, experts):
    local, _, hidden = weights[0].shape
    part = jax.ShapeDtypeStruct((2, local, 3, len(tokens) * capacity, hidden // 4), BF16)
    return call(
        functools.partial(first_kernel, len(tokens), experts, capacity),
        [plan, *tokens, *weights],
        [pl.BlockSpec(memory_space=pltpu.SMEM)]
        + in_vmem(len(tokens))
        + [pl.BlockSpec(memory_space=pltpu.HBM)] * 3,
        [part, part] + [jax.ShapeDtypeStruct(w.shape, w.dtype) for w in weights],
        in_vmem(5),
        scratch=[pltpu.SemaphoreType.DMA((3 * local,))],
        limit=FIRST_VMEM_LIMIT,
        name="first_products",
    )


def slot_rows(plan_ref, expert, experts, capacity, token_refs):
    width = (token_refs[0].shape[1] - META) // 2
    tokens = token_refs[0].shape[0]
    lane = lax.broadcasted_iota(jnp.int32, (16, META), 1)
    pick = jnp.where(lane == 2 * experts + plan_ref[0] + expert, 1.0, 0.0).astype(BF16)
    slot = lax.broadcasted_iota(jnp.int32, (capacity, tokens), 0)
    parts_in, parts_grad = [], []
    for token_ref in token_refs:
        slot_of = dot_t(pick, token_ref[:, 2 * width :])[0:1, :].astype(jnp.int32)
        chosen = jnp.where(slot == slot_of, 1.0, 0.0).astype(BF16)
        parts_in.append(dot(chosen, token_ref[:, :width]).astype(BF16))
        parts_grad.append(dot(chosen, token_ref[:, width : 2 * width]).astype(BF16))
    return jnp.concatenate(parts_in, axis=0), jnp.concatenate(parts_grad, axis=0)


def columns(plan_ref, place, quarter):
    return pl.ds(pl.multiple_of(plan_ref[place] * quarter, quarter), quarter)


def products_kernel(blocks, experts, capacity, plan_ref, *refs):
    token_refs = refs[:blocks]
    gate_ref, up_ref, down_ref, send_ref, keep_ref = refs[blocks:]
    local = gate_ref.shape[0]
    quarter = gate_ref.shape[2] // 4
    rows = [slot_rows(plan_ref, e, experts, capacity, token_refs) for e in range(local)]
    for place, out_ref in ((1, send_ref), (3, keep_ref)):
        for j in range(2):
            part = columns(plan_ref, place + j, quarter)
            for e in range(local):
                out_ref[j, e, 0] = dot(rows[e][0], gate_ref[e, :, part]).astype(BF16)
                out_ref[j, e, 1] = dot(rows[e][0], up_ref[e, :, part]).astype(BF16)
                out_ref[j, e, 2] = dot_t(rows[e][1], down_ref[e, part, :]).astype(BF16)


def in_vmem(count):
    return [pl.BlockSpec(memory_space=pltpu.VMEM)] * count


def products(plan, tokens, w_gate, w_up, w_down, capacity, experts, deps):
    local, _, hidden = w_gate.shape
    slots = len(tokens) * capacity
    shape = jax.ShapeDtypeStruct((2, local, 3, slots, hidden // 4), BF16)
    return call(
        functools.partial(products_kernel, len(tokens), experts, capacity),
        [plan, *tokens, w_gate, w_up, w_down],
        [pl.BlockSpec(memory_space=pltpu.SMEM)] + in_vmem(len(tokens) + 3),
        [shape, shape],
        in_vmem(2),
        deps,
        name="products",
    )


def add_kernel(*refs):
    *terms, out_ref = refs
    value = terms[0][...].astype(F32)
    for term in terms[1:]:
        value = value + term[...].astype(F32)
    out_ref[...] = value.astype(out_ref.dtype)


def part_spec(part, shape):
    zeros = (0,) * (len(shape) - 1)
    return pl.BlockSpec((None, *shape[1:]), lambda i: (part, *zeros))


def add_parts(terms, dtype, deps=()):
    shape = terms[0][0].shape[1:]
    return call(
        add_kernel,
        [term for term, _ in terms],
        [part_spec(part, term.shape) for term, part in terms],
        jax.ShapeDtypeStruct(shape, dtype),
        pl.BlockSpec(shape, lambda i: (0,) * len(shape)),
        deps,
        grid=(1,),
        name="add_parts",
    )


def back_kernel(got_ref, kept_ref, other_ref, out_ref):
    for e in range(out_ref.shape[0]):
        gate_pre, up_pre, hidden_grad = (
            got_ref[0, e, m].astype(F32) + kept_ref[0, e, m].astype(F32) + other_ref[e, m].astype(F32)
            for m in range(3)
        )
        out_ref[e, 0], out_ref[e, 1] = swiglu_back(gate_pre, up_pre, hidden_grad)


def hidden_back(got, kept, other, deps):
    _, local, _, slots, quarter = got.shape
    last = pl.BlockSpec((1, local, 3, slots, quarter), lambda i: (1, 0, 0, 0, 0))
    return call(
        back_kernel,
        [got, kept, other],
        [last, last, pl.BlockSpec((local, 3, slots, quarter), lambda i: (0, 0, 0, 0))],
        jax.ShapeDtypeStruct((local, 2, slots, quarter), BF16),
        pl.BlockSpec((local, 2, slots, quarter), lambda i: (0, 0, 0, 0)),
        deps,
        grid=(1,),
        name="hidden_back",
    )


def join_kernel(own_ref, other_ref, out_ref):
    out_ref[0] = own_ref[...]
    out_ref[1] = other_ref[...]


def join(own, other, deps):
    shape = jax.ShapeDtypeStruct((2, *own.shape), own.dtype)
    return call(join_kernel, [own, other], in_vmem(2), shape, in_vmem(1)[0], deps, name="join")


def route_kernel(blocks, mine, experts, capacity, plan_ref, *refs):
    meta_refs, refs = refs[:blocks], refs[blocks:]
    piece_refs, (gate_ref, up_ref), out_refs = refs[:2], refs[2:4], refs[4:]
    local = gate_ref.shape[0]
    quarter = gate_ref.shape[2] // 4
    tokens = meta_refs[0].shape[0]
    row = lax.broadcasted_iota(jnp.int32, (META, META), 0)
    lane = lax.broadcasted_iota(jnp.int32, (META, META), 1)
    slot = lax.broadcasted_iota(jnp.int32, (tokens, capacity), 1)
    totals = [None] * blocks
    for e in range(local):
        route = None
        for p in range(4):
            piece_ref = piece_refs[p // 2]
            part = columns(plan_ref, 5 + p, quarter)
            value = dot_t(piece_ref[p % 2, e, 0], gate_ref[e, :, part])
            value = value + dot_t(piece_ref[p % 2, e, 1], up_ref[e, :, part])
            route = value if route is None else route + value
        route = route.astype(BF16)
        pick = jnp.where(lane == row * experts + plan_ref[0] + e, 1.0, 0.0).astype(BF16)
        for b in range(blocks):
            found = dot_t(meta_refs[b][...], pick)
            named = found[:, 2:3].astype(jnp.int32) == slot
            high = jnp.where(named, found[:, 0:1], 0.0).astype(BF16)
            low = jnp.where(named, found[:, 1:2], 0.0).astype(BF16)
            own = route[b * capacity : (b + 1) * capacity, :]
            value = dot(high, own) + dot(low, own)
            totals[b] = value if totals[b] is None else totals[b] + value
    out_refs = list(out_refs)
    if mine:
        mine_ref = out_refs.pop(0)
        for b in range(mine):
            mine_ref[b] = totals[b]
    for b in range(mine, blocks):
        out_refs[0][b - mine] = totals[b].astype(BF16)


def route_sums(plan, tokens, mine, pieces, w_gate, w_up, capacity, experts, deps):
    width = w_gate.shape[1]
    blocks = len(tokens)
    count = tokens[0].shape[0]
    meta_at = 2 * width // META
    out_shape = []
    if mine:
        out_shape.append(jax.ShapeDtypeStruct((mine, count, width), F32))
    if blocks > mine:
        out_shape.append(jax.ShapeDtypeStruct((blocks - mine, count, width), BF16))
    return call(
        functools.partial(route_kernel, blocks, mine, experts, capacity),
        [plan, *tokens, *pieces, w_gate, w_up],
        [pl.BlockSpec(memory_space=pltpu.SMEM)]
        + [pl.BlockSpec((count, META), lambda i: (0, meta_at))] * blocks
        + in_vmem(4),
        out_shape,
        in_vmem(len(out_shape)),
        deps,
        grid=(1,),
        name="route_sums",
    )


def plane_shift(value, near, name):
    count = lax.axis_size("exp")
    pairs = []
    for c in range(lax.axis_size("ctx")):
        for i in range(count):
            bits = 1 if (i % 2 == 0) == near else 2
            pairs.append((c * count + i, (c ^ bits) * count + i))
    with jax.named_scope(name):
        return lax.ppermute(value, ("ctx", "exp"), pairs)


class Chunk:
    def __init__(self, name, plan, weights, capacity, experts, mine):
        self.name, self.plan, self.weights, self.mine = name, plan, weights, mine
        self.capacity, self.experts = capacity, experts

    def multiply(self, tokens, *deps):
        return self.begin(
            tokens, *products(self.plan, tokens, *self.weights, self.capacity, self.experts, deps)
        )

    def begin(self, tokens, send, kept):
        self.tokens, self.kept = tokens, kept
        self.got = plane_shift(send, True, self.name + "_sums_near")
        return kept

    def add(self, *deps):
        half = add_parts([(self.got, 0), (self.kept, 0)], BF16, deps)
        self.other = plane_shift(half, False, self.name + "_sums_far")
        return half

    def turn(self, *deps):
        self.own = hidden_back(self.got, self.kept, self.other, deps)
        self.from_far = plane_shift(self.own, False, self.name + "_own_far")
        return self.own

    def forward(self, *deps):
        self.joined = join(self.own, self.from_far, deps)
        self.from_near = plane_shift(self.joined, True, self.name + "_both_near")
        return self.joined

    def finish(self, *deps):
        return route_sums(
            self.plan,
            self.tokens,
            self.mine,
            [self.joined, self.from_near],
            *self.weights[:2],
            self.capacity,
            self.experts,
            deps,
        )


def near_layers(
    moe_input, moe_grad, routes, gates, w_gate, w_up, w_down, queries, out_grad, positions, latents
):
    tok_rows = moe_input.shape[0]
    fanout = routes.shape[1]
    local = w_gate.shape[0]
    exp_count = lax.axis_size("exp")
    experts = local * exp_count
    capacity = tok_rows * fanout // experts * 5 // 4
    ctx, exp = lax.axis_index("ctx"), lax.axis_index("exp")
    x, y = ctx % 2, ctx // 2
    near = jnp.where(exp % 2 == 0, x, y)
    far = jnp.where(exp % 2 == 0, y, x)
    near_bit = jnp.where(exp % 2 == 0, 1, 2)
    plan = jnp.stack(
        [
            exp * local,
            (1 - near) * 2 + 1 - far,
            (1 - near) * 2 + far,
            near * 2 + 1 - far,
            near * 2 + far,
            near * 2 + far,
            near * 2 + 1 - far,
            (1 - near) * 2 + far,
            (1 - near) * 2 + 1 - far,
            exp,
            ctx,
            ctx ^ (3 - near_bit),
            ctx ^ near_bit,
            ctx ^ 3,
        ]
    ).astype(jnp.int32)

    def chunk(name, mine):
        return Chunk(name, plan, weights, capacity, experts, mine)

    own = pack_tokens(moe_input, moe_grad, routes, gates, experts)
    partner = shift(own, 1, "partner_move")
    first = [own, partner]
    LENGTH[0] = 10
    send, kept, *weights = first_products(plan, first, (w_gate, w_up, w_down), capacity, experts)
    a = chunk("a", 1)
    from_1 = shift(own, 2, "from_1_move")
    from_3 = shift(own, 6, "from_3_move")
    other_1 = shift(from_1, 1, "other_1_move")
    other_3 = shift(from_3, 1, "other_3_move")
    from_2 = shift(from_3, 2, "from_2_move")
    other_2 = shift(from_2, 1, "other_2_move")
    keys = latents.T
    keys_near = plane_shift(keys, True, "keys_near_move")
    keys_far = plane_shift(keys, False, "keys_far_move")
    keys_both = plane_shift(keys_near, False, "keys_both_move")
    made = {}

    def attend(*deps):
        made["queries"], give, made["keep"] = attention(
            plan, queries, out_grad, positions, [keys, keys_far, keys_near, keys_both], deps
        )
        made["got"] = shift(give, 1, "got_move")
        return made["keep"]

    def latent_cores(*deps):
        made["cores"] = both = add_parts([(made["keep"][None], 0), (made["got"][None], 0)], BF16, deps)
        made["terms"] = [shift(both[i], 2 * i, "latent_terms") for i in range(1, exp_count // 2)]
        return both

    def latent_chips(*deps):
        terms = [(made["cores"], 0)] + [(term[None], 0) for term in made["terms"]]
        made["chips"] = both = add_parts(terms, BF16, deps)
        made["crossed"] = plane_shift(both[2:], True, "crossed_move")
        return both

    def latent_near(*deps):
        terms = [(made["chips"][None, :2], 0), (made["crossed"][None], 0)]
        made["pair"] = both = add_parts(terms, BF16, deps)
        made["last"] = plane_shift(both[1], False, "last_move")
        return both

    def latent_far(*deps):
        terms = [(made["pair"], 0), (made["last"][None], 0)]
        made["latents"] = add_parts(terms, F32, deps)
        return made["latents"]

    def start_total(*deps):
        made["total"], theirs = a.finish(*deps)
        made["more"] = [(shift(theirs, 1, "a_other_move"), 0)]
        return theirs

    def finish(chunk):
        def act(*deps):
            *mine, theirs = chunk.finish(*deps)
            made[chunk.name] = mine
            made[chunk.name + "_other"] = shift(theirs, 1, chunk.name + "_other_move")
            return theirs

        return act

    def send_back(chunk, bits):
        def act(*deps):
            made[chunk.name + "_back"] = []
            for place, bit in enumerate(bits):
                terms = [(made[chunk.name][0], place), (made[chunk.name + "_other"], place)]
                both = add_parts(terms, BF16, deps)
                back = shift(both, bit, chunk.name + "_back_move")
                made[chunk.name + "_back"].append((back[None], 0))
            return both

        return act

    def receive(chunk, last):
        def act(*deps):
            terms = [(made["total"], 0)] + made.pop("more", []) + made[chunk.name + "_back"]
            total = add_parts(terms, BF16 if last else F32, deps)
            made["total"] = total[None]
            return total

        return act

    b = chunk("b", 1)
    c = chunk("c", 1)
    d = chunk("d", 1)
    order = (
        (functools.partial(b.multiply, [from_1, other_1]), 2),
        (a.add, 2),
        (a.turn, 2),
        (attend, 2),
        (a.forward, 2),
        (b.add, 2),
        (start_total, 2),
        (functools.partial(c.multiply, [from_3, other_3]), 2),
        (b.turn, 2, from_2),
        (latent_cores, 2),
        (b.forward, 2),
        (c.add, 2),
        (functools.partial(d.multiply, [from_2, other_2]), 2),
        (finish(b), 2),
        (latent_chips, 2),
        (c.turn, 0),
        (send_back(b, (2,)), 2),
        (d.add, 2),
        (c.forward, 2),
        (latent_near, 2),
        (d.turn, 2),
        (finish(c), 2),
        (receive(b, False), 2),
        (d.forward, 2),
        (send_back(c, (6,)), 2),
        (latent_far, 2),
        (finish(d), 2),
        (receive(c, False), 2),
        (send_back(d, (4,)), 2),
        (receive(d, True), 2),
    )
    step = a.begin(first, send, kept)
    for act, length, *waits in order:
        LENGTH[0] = length
        step = act(step, *waits)
    return (made["total"][0], made["queries"], made["latents"])


def attention_kernel(heads, plan_ref, queries_ref, grads_ref, positions_ref, *refs):
    key_refs, (query_ref, give_ref, keep_ref, total_ref) = refs[:4], refs[4:]
    rows = queries_ref.shape[0]
    width, keys = key_refs[0].shape
    values = grads_ref.shape[1] // heads
    chips, shards, own_keys, _ = give_ref.shape
    square = lax.broadcasted_iota(jnp.int32, (rows, rows), 0)
    diagonal = square == lax.broadcasted_iota(jnp.int32, (rows, rows), 1)
    position = jnp.sum(
        jnp.where(diagonal, positions_ref[...].astype(F32), 0.0), axis=1, keepdims=True
    ).astype(jnp.int32)
    offset = lax.broadcasted_iota(jnp.int32, (rows, keys), 1)
    visible = [offset + plan_ref[10 + r] * keys <= position for r in range(shards)]
    outs = []
    for h in range(heads):
        query = queries_ref[:, h * width : (h + 1) * width]
        grad = grads_ref[:, h * values : (h + 1) * values]
        scores = [
            jnp.where(visible[r], dot(query, key_refs[r][...]) * SCORE_SCALE, MASKED)
            for r in range(shards)
        ]
        peak = functools.reduce(jnp.maximum, scores)
        peak = jnp.max(peak, axis=1, keepdims=True)
        raw = [jnp.where(visible[r], jnp.exp(scores[r] - peak), 0.0) for r in range(shards)]
        whole = jnp.sum(functools.reduce(jnp.add, raw), axis=1, keepdims=True)
        attend = [part / whole for part in raw]
        value_dot = [dot(grad, key_refs[r][:values, :]) for r in range(shards)]
        row_dot = functools.reduce(jnp.add, [a * v for a, v in zip(attend, value_dot)])
        row_dot = jnp.sum(row_dot, axis=1, keepdims=True)
        query_grad = None
        for r in range(shards):
            score_grad = (attend[r] * (value_dot[r] - row_dot)).astype(BF16)
            term = dot_t(score_grad, key_refs[r][...])
            query_grad = term if query_grad is None else query_grad + term
            key_grad = dot_rows(score_grad, query) * SCORE_SCALE
            value_grad = dot_rows(attend[r].astype(BF16), grad)
            part = pl.ds(r * keys, keys)
            if h == 0:
                total_ref[part, :] = key_grad
            else:
                total_ref[part, :] += key_grad
            total_ref[part, :values] += value_grad
        outs.append((query_grad * SCORE_SCALE).astype(BF16))
    query_ref[...] = jnp.concatenate(outs, axis=1)
    core, chip = plan_ref[9] % 2, plan_ref[9] // 2
    for b in range(chips):
        for r in range(shards):
            start = r * keys + (chip ^ b) * (2 * own_keys)
            across = (r % 2) * 2 + r // 2
            for out_ref, which, place in ((give_ref, 1 - core, across), (keep_ref, core, r)):
                at = pl.multiple_of(start + which * own_keys, own_keys)
                out_ref[b, place] = total_ref[pl.ds(at, own_keys), :].astype(BF16)


def dot_rows(left, right):
    return lax.dot_general(left, right, (((0,), (0,)), ((), ())), preferred_element_type=F32)


def attention(plan, queries, out_grad, positions, keys, deps):
    rows = queries.shape[0]
    width, count = keys[0].shape
    heads = queries.shape[1] // width
    exp_count = lax.axis_size("exp")
    terms = jax.ShapeDtypeStruct((exp_count // 2, len(keys), count // exp_count, width), BF16)
    return call(
        functools.partial(attention_kernel, heads),
        [plan, queries, out_grad, positions.reshape(1, rows), *keys],
        [pl.BlockSpec(memory_space=pltpu.SMEM)] + in_vmem(3 + len(keys)),
        [jax.ShapeDtypeStruct(queries.shape, BF16), terms, terms],
        in_vmem(3),
        deps,
        scratch=[pltpu.VMEM((len(keys) * count, width), F32)],
        name="attention",
    )


def far_expert_layer(moe_input, moe_grad, routes, gates, w_gate, w_up, w_down):
    tok_rows, width_part = moe_input.shape
    fanout = routes.shape[1]
    local_experts = w_gate.shape[0]
    exp_count = lax.axis_size("exp")
    experts = local_experts * exp_count
    capacity = tok_rows * fanout // experts * 5 // 4
    flat_routes = routes.reshape(-1)
    onehot = (flat_routes[:, None] == jnp.arange(experts, dtype=jnp.int32)[None, :]).astype(
        jnp.int32
    )
    before = jnp.cumsum(onehot, axis=0) - onehot
    slot_index = jnp.sum(before * onehot, axis=1)
    target = flat_routes * capacity + slot_index
    source_rows = jnp.arange(tok_rows * fanout, dtype=jnp.int32) // fanout
    empty = jnp.zeros((experts * capacity, width_part), BF16)
    send_shape = (exp_count, local_experts * capacity, width_part)
    send_input = empty.at[target].set(moe_input[source_rows]).reshape(send_shape)
    send_grad = empty.at[target].set(moe_grad[source_rows]).reshape(send_shape)
    recv_input, recv_grad = (
        lax.all_to_all(send_input, "exp", split_axis=0, concat_axis=0, tiled=True),
        lax.all_to_all(send_grad, "exp", split_axis=0, concat_axis=0, tiled=True),
    )
    slot_shape = (exp_count, local_experts, capacity, width_part)
    recv_input = recv_input.reshape(slot_shape)
    recv_grad = recv_grad.reshape(slot_shape)
    gate_part = jnp.einsum("sekd,edh->sekh", recv_input, w_gate, preferred_element_type=F32)
    up_part = jnp.einsum("sekd,edh->sekh", recv_input, w_up, preferred_element_type=F32)
    down_part = jnp.einsum("sekd,ehd->sekh", recv_grad, w_down, preferred_element_type=F32)
    gate_pre, up_pre, hidden_grad = (
        lax.psum(gate_part.astype(BF16), "ctx").astype(F32),
        lax.psum(up_part.astype(BF16), "ctx").astype(F32),
        lax.psum(down_part.astype(BF16), "ctx").astype(F32),
    )
    gate_back, up_back = swiglu_back(gate_pre, up_pre, hidden_grad)
    route_part = jnp.einsum("sekh,edh->sekd", gate_back, w_gate, preferred_element_type=F32)
    route_part = route_part + jnp.einsum(
        "sekh,edh->sekd", up_back, w_up, preferred_element_type=F32
    )
    route_part = route_part.astype(BF16).reshape(send_shape)
    returned = lax.all_to_all(route_part, "exp", split_axis=0, concat_axis=0, tiled=True).reshape(
        experts * capacity, width_part
    )
    per_route = returned[target].reshape(tok_rows, fanout, width_part).astype(F32)
    return jnp.sum(per_route * gates[:, :, None], axis=1).astype(BF16)


def sum_latent_grad(part):
    keys, width = part.shape
    shards, exp_count = lax.axis_size("ctx"), lax.axis_size("exp")
    part = part.reshape(shards, exp_count, keys // shards // exp_count, width).swapaxes(0, 1)
    part = part.reshape(keys, width).astype(BF16)
    part = lax.psum_scatter(part, "exp", scatter_dimension=0, tiled=True)
    return lax.psum_scatter(part.astype(F32), "ctx", scatter_dimension=0, tiled=True)


def attention_layer(queries, out_grad, positions, latents):
    q_rows = queries.shape[0]
    lat_width = latents.shape[1]
    head_count = queries.shape[1] // lat_width
    val_width = out_grad.shape[1] // head_count
    query_heads = queries.reshape(q_rows, head_count, lat_width)
    grad_heads = out_grad.reshape(q_rows, head_count, val_width)
    gathered = lax.all_gather(latents, "ctx", axis=0, tiled=True)
    key_ids = jnp.arange(gathered.shape[0], dtype=jnp.int32)
    visible = (key_ids[None, :] <= positions[:, None])[None]
    scores = (
        jnp.einsum("qhc,kc->hqk", query_heads, gathered, preferred_element_type=F32) * SCORE_SCALE
    )
    scores = jnp.where(visible, scores, MASKED)
    peak = jnp.max(scores, axis=2, keepdims=True)
    raw = jnp.where(visible, jnp.exp(scores - peak), 0.0)
    attend = raw / jnp.sum(raw, axis=2, keepdims=True)
    value_dot = jnp.einsum(
        "qhv,kv->hqk", grad_heads, gathered[:, :val_width], preferred_element_type=F32
    )
    row_dot = jnp.sum(attend * value_dot, axis=2, keepdims=True)
    score_grad = (attend * (value_dot - row_dot)).astype(BF16)
    query_grad = (
        jnp.einsum("hqk,kc->qhc", score_grad, gathered, preferred_element_type=F32) * SCORE_SCALE
    )
    key_grad = (
        jnp.einsum("hqk,qhc->kc", score_grad, query_heads, preferred_element_type=F32)
        * SCORE_SCALE
    )
    value_grad = jnp.einsum(
        "hqk,qhv->kv", attend.astype(BF16), grad_heads, preferred_element_type=F32
    )
    latent_part = key_grad + jnp.pad(value_grad, ((0, 0), (0, lat_width - val_width)))
    latent_grad = sum_latent_grad(latent_part)
    query_out = query_grad.astype(BF16).reshape(q_rows, head_count * lat_width)
    return (query_out, latent_grad)


def per_device(
    moe_input, moe_grad, routes, gates, w_gate, w_up, w_down, queries, out_grad, positions, latents
):
    if lax.axis_size("exp") <= routes.shape[1]:
        return near_layers(
            moe_input, moe_grad, routes, gates, w_gate, w_up, w_down,
            queries, out_grad, positions, latents,
        )
    query_out, latent_grad = attention_layer(queries, out_grad, positions, latents)
    input_grad = far_expert_layer(moe_input, moe_grad, routes, gates, w_gate, w_up, w_down)
    return (input_grad, query_out, latent_grad)


def solution(mesh):
    return jax.shard_map(
        per_device,
        mesh=mesh,
        in_specs=(
            P("exp", "ctx"),
            P("exp", "ctx"),
            P("exp", None),
            P("exp", None),
            P("exp", "ctx", None),
            P("exp", "ctx", None),
            P("exp", None, "ctx"),
            P("ctx", "exp"),
            P("ctx", "exp"),
            P("ctx"),
            P("ctx", None),
        ),
        out_specs=(P("exp", "ctx"), P("ctx", "exp"), P(("ctx", "exp"), None)),
        check_vma=False,
    )
```

```python
import functools

import jax
import jax.numpy as jnp
from jax import lax
from jax.experimental import pallas as pl
from jax.experimental.pallas import tpu as pltpu
from jax.sharding import PartitionSpec as P

SCORE_SCALE = 192.0 ** (-0.5)
MASKED = -1e30
BF16 = jnp.bfloat16
F32 = jnp.float32
META = 128
VMEM_LIMIT = 16 * 1024 * 1024
AHEAD = 3
FIRST_VMEM_LIMIT = 40 * 10**6


def swiglu_back(gate_pre, up_pre, hidden_grad):
    sigma = jax.nn.sigmoid(gate_pre)
    gate_back = hidden_grad * up_pre * sigma * (1.0 + gate_pre * (1.0 - sigma))
    up_back = hidden_grad * gate_pre * sigma
    return (gate_back.astype(BF16), up_back.astype(BF16))


def shift(value, bits, name):
    pairs = [(i, i ^ bits) for i in range(lax.axis_size("exp"))]
    with jax.named_scope(name):
        return lax.ppermute(value, "exp", pairs)


def declared(length):
    return pl.CostEstimate(
        flops=int(length * 10**9) + 1, bytes_accessed=int(length * 3 * 10**6) + 1, transcendentals=0
    )


LENGTH = [1]


def call(kernel, args, in_specs, out_shape, out_specs, deps=(), grid=(), scratch=(), limit=None, name=None):
    count = len(args)

    def body(*refs):
        kernel(*refs[:count], *refs[count + len(deps) :])

    return pl.pallas_call(
        body,
        out_shape=out_shape,
        grid=grid,
        in_specs=list(in_specs) + [pl.BlockSpec(memory_space=pl.ANY)] * len(deps),
        out_specs=out_specs,
        scratch_shapes=scratch,
        compiler_params=pltpu.CompilerParams(vmem_limit_bytes=limit or VMEM_LIMIT),
        cost_estimate=declared(LENGTH[0]),
        name=name,
    )(*args, *deps)


def dot(left, right):
    return jnp.dot(left, right, preferred_element_type=F32)


def dot_t(left, right):
    return lax.dot_general(left, right, (((1,), (1,)), ((), ())), preferred_element_type=F32)


def pack(experts, routes, gates, rows_in, rows_grad, out_ref):
    rows, width = rows_in.shape
    out_ref[:, :width] = rows_in
    out_ref[:, width : 2 * width] = rows_grad
    lane = lax.broadcasted_iota(jnp.int32, (rows, META), 1)
    expert = lane % experts
    section = lane // experts
    gate = jnp.zeros((rows, META), F32)
    named = jnp.zeros((rows, META), F32)
    for k in range(routes.shape[1]):
        hit = routes[:, k : k + 1] == expert
        gate = gate + jnp.where(hit, gates[:, k : k + 1], 0.0)
        named = named + jnp.where(hit, 1.0, 0.0)
    low = lax.broadcasted_iota(jnp.int32, (rows, rows), 0)
    high = lax.broadcasted_iota(jnp.int32, (rows, rows), 1)
    before = jnp.where(high < low, 1.0, 0.0).astype(BF16)
    slot = jnp.where(named > 0.0, dot(before, named.astype(BF16)), -1.0)
    gate_high = gate.astype(BF16).astype(F32)
    meta = jnp.where(section == 0, gate_high, jnp.where(section == 1, gate - gate_high, slot))
    out_ref[:, 2 * width :] = meta.astype(BF16)


def pack_kernel(experts, routes_ref, gates_ref, input_ref, grad_ref, out_ref):
    pack(experts, routes_ref[...].T, gates_ref[...].T, input_ref[...], grad_ref[...], out_ref)


def pack_tokens(moe_input, moe_grad, routes, gates, experts):
    rows, width = moe_input.shape
    return call(
        functools.partial(pack_kernel, experts),
        [routes.T, gates.T, moe_input, moe_grad],
        in_vmem(4),
        jax.ShapeDtypeStruct((rows, 2 * width + META), BF16),
        in_vmem(1)[0],
        name="pack_tokens",
    )


def first_kernel(blocks, experts, capacity, plan_ref, *refs):
    token_refs, args, refs = refs[:blocks], refs[blocks : blocks + 3], refs[blocks + 3 :]
    send_ref, keep_ref = refs[:2]
    weights, sem = refs[2:5], refs[5]
    local = weights[0].shape[0]
    quarter = weights[0].shape[2] // 4
    copies = [
        pltpu.make_async_copy(args[m].at[e], weights[m].at[e], sem.at[3 * e + m])
        for e in range(local)
        for m in range(3)
    ]
    for copy in copies[:AHEAD]:
        copy.start()
    for e in range(local):
        rows = slot_rows(plan_ref, e, experts, capacity, token_refs)
        for m in range(3):
            copies[3 * e + m].wait()
            if 3 * e + m + AHEAD < len(copies):
                copies[3 * e + m + AHEAD].start()
            for place, out_ref in ((1, send_ref), (3, keep_ref)):
                for j in range(2):
                    part = columns(plan_ref, place + j, quarter)
                    if m < 2:
                        value = dot(rows[0], weights[m][e, :, part])
                    else:
                        value = dot_t(rows[1], weights[m][e, part, :])
                    out_ref[j, e, m] = value.astype(BF16)


def first_products(plan, tokens, weights, capacity, experts):
    local, _, hidden = weights[0].shape
    part = jax.ShapeDtypeStruct((2, local, 3, len(tokens) * capacity, hidden // 4), BF16)
    return call(
        functools.partial(first_kernel, len(tokens), experts, capacity),
        [plan, *tokens, *weights],
        [pl.BlockSpec(memory_space=pltpu.SMEM)]
        + in_vmem(len(tokens))
        + [pl.BlockSpec(memory_space=pltpu.HBM)] * 3,
        [part, part] + [jax.ShapeDtypeStruct(w.shape, w.dtype) for w in weights],
        in_vmem(5),
        scratch=[pltpu.SemaphoreType.DMA((3 * local,))],
        limit=FIRST_VMEM_LIMIT,
        name="first_products",
    )


def slot_rows(plan_ref, expert, experts, capacity, token_refs):
    width = (token_refs[0].shape[1] - META) // 2
    tokens = token_refs[0].shape[0]
    lane = lax.broadcasted_iota(jnp.int32, (16, META), 1)
    pick = jnp.where(lane == 2 * experts + plan_ref[0] + expert, 1.0, 0.0).astype(BF16)
    slot = lax.broadcasted_iota(jnp.int32, (capacity, tokens), 0)
    parts_in, parts_grad = [], []
    for token_ref in token_refs:
        slot_of = dot_t(pick, token_ref[:, 2 * width :])[0:1, :].astype(jnp.int32)
        chosen = jnp.where(slot == slot_of, 1.0, 0.0).astype(BF16)
        parts_in.append(dot(chosen, token_ref[:, :width]).astype(BF16))
        parts_grad.append(dot(chosen, token_ref[:, width : 2 * width]).astype(BF16))
    return jnp.concatenate(parts_in, axis=0), jnp.concatenate(parts_grad, axis=0)


def columns(plan_ref, place, quarter):
    return pl.ds(pl.multiple_of(plan_ref[place] * quarter, quarter), quarter)


def products_kernel(blocks, experts, capacity, plan_ref, *refs):
    token_refs = refs[:blocks]
    gate_ref, up_ref, down_ref, send_ref, keep_ref = refs[blocks:]
    local = gate_ref.shape[0]
    quarter = gate_ref.shape[2] // 4
    rows = [slot_rows(plan_ref, e, experts, capacity, token_refs) for e in range(local)]
    for place, out_ref in ((1, send_ref), (3, keep_ref)):
        for j in range(2):
            part = columns(plan_ref, place + j, quarter)
            for e in range(local):
                out_ref[j, e, 0] = dot(rows[e][0], gate_ref[e, :, part]).astype(BF16)
                out_ref[j, e, 1] = dot(rows[e][0], up_ref[e, :, part]).astype(BF16)
                out_ref[j, e, 2] = dot_t(rows[e][1], down_ref[e, part, :]).astype(BF16)


def in_vmem(count):
    return [pl.BlockSpec(memory_space=pltpu.VMEM)] * count


def products(plan, tokens, w_gate, w_up, w_down, capacity, experts, deps):
    local, _, hidden = w_gate.shape
    slots = len(tokens) * capacity
    shape = jax.ShapeDtypeStruct((2, local, 3, slots, hidden // 4), BF16)
    return call(
        functools.partial(products_kernel, len(tokens), experts, capacity),
        [plan, *tokens, w_gate, w_up, w_down],
        [pl.BlockSpec(memory_space=pltpu.SMEM)] + in_vmem(len(tokens) + 3),
        [shape, shape],
        in_vmem(2),
        deps,
        name="products",
    )


def add_kernel(*refs):
    *terms, out_ref = refs
    value = terms[0][...].astype(F32)
    for term in terms[1:]:
        value = value + term[...].astype(F32)
    out_ref[...] = value.astype(out_ref.dtype)


def part_spec(part, shape):
    zeros = (0,) * (len(shape) - 1)
    return pl.BlockSpec((None, *shape[1:]), lambda i: (part, *zeros))


def add_parts(terms, dtype, deps=()):
    shape = terms[0][0].shape[1:]
    return call(
        add_kernel,
        [term for term, _ in terms],
        [part_spec(part, term.shape) for term, part in terms],
        jax.ShapeDtypeStruct(shape, dtype),
        pl.BlockSpec(shape, lambda i: (0,) * len(shape)),
        deps,
        grid=(1,),
        name="add_parts",
    )


def back_kernel(got_ref, kept_ref, other_ref, out_ref):
    for e in range(out_ref.shape[0]):
        gate_pre, up_pre, hidden_grad = (
            got_ref[0, e, m].astype(F32) + kept_ref[0, e, m].astype(F32) + other_ref[e, m].astype(F32)
            for m in range(3)
        )
        out_ref[e, 0], out_ref[e, 1] = swiglu_back(gate_pre, up_pre, hidden_grad)


def hidden_back(got, kept, other, deps):
    _, local, _, slots, quarter = got.shape
    last = pl.BlockSpec((1, local, 3, slots, quarter), lambda i: (1, 0, 0, 0, 0))
    return call(
        back_kernel,
        [got, kept, other],
        [last, last, pl.BlockSpec((local, 3, slots, quarter), lambda i: (0, 0, 0, 0))],
        jax.ShapeDtypeStruct((local, 2, slots, quarter), BF16),
        pl.BlockSpec((local, 2, slots, quarter), lambda i: (0, 0, 0, 0)),
        deps,
        grid=(1,),
        name="hidden_back",
    )


def join_kernel(own_ref, other_ref, out_ref):
    out_ref[0] = own_ref[...]
    out_ref[1] = other_ref[...]


def join(own, other, deps):
    shape = jax.ShapeDtypeStruct((2, *own.shape), own.dtype)
    return call(join_kernel, [own, other], in_vmem(2), shape, in_vmem(1)[0], deps, name="join")


def route_kernel(blocks, mine, experts, capacity, plan_ref, *refs):
    meta_refs, refs = refs[:blocks], refs[blocks:]
    piece_refs, (gate_ref, up_ref), out_refs = refs[:2], refs[2:4], refs[4:]
    local = gate_ref.shape[0]
    quarter = gate_ref.shape[2] // 4
    tokens = meta_refs[0].shape[0]
    row = lax.broadcasted_iota(jnp.int32, (META, META), 0)
    lane = lax.broadcasted_iota(jnp.int32, (META, META), 1)
    slot = lax.broadcasted_iota(jnp.int32, (tokens, capacity), 1)
    totals = [None] * blocks
    for e in range(local):
        route = None
        for p in range(4):
            piece_ref = piece_refs[p // 2]
            part = columns(plan_ref, 5 + p, quarter)
            value = dot_t(piece_ref[p % 2, e, 0], gate_ref[e, :, part])
            value = value + dot_t(piece_ref[p % 2, e, 1], up_ref[e, :, part])
            route = value if route is None else route + value
        route = route.astype(BF16)
        pick = jnp.where(lane == row * experts + plan_ref[0] + e, 1.0, 0.0).astype(BF16)
        for b in range(blocks):
            found = dot_t(meta_refs[b][...], pick)
            named = found[:, 2:3].astype(jnp.int32) == slot
            high = jnp.where(named, found[:, 0:1], 0.0).astype(BF16)
            low = jnp.where(named, found[:, 1:2], 0.0).astype(BF16)
            own = route[b * capacity : (b + 1) * capacity, :]
            value = dot(high, own) + dot(low, own)
            totals[b] = value if totals[b] is None else totals[b] + value
    out_refs = list(out_refs)
    if mine:
        mine_ref = out_refs.pop(0)
        for b in range(mine):
            mine_ref[b] = totals[b]
    for b in range(mine, blocks):
        out_refs[0][b - mine] = totals[b].astype(BF16)


def route_sums(plan, tokens, mine, pieces, w_gate, w_up, capacity, experts, deps):
    width = w_gate.shape[1]
    blocks = len(tokens)
    count = tokens[0].shape[0]
    meta_at = 2 * width // META
    out_shape = []
    if mine:
        out_shape.append(jax.ShapeDtypeStruct((mine, count, width), F32))
    if blocks > mine:
        out_shape.append(jax.ShapeDtypeStruct((blocks - mine, count, width), BF16))
    return call(
        functools.partial(route_kernel, blocks, mine, experts, capacity),
        [plan, *tokens, *pieces, w_gate, w_up],
        [pl.BlockSpec(memory_space=pltpu.SMEM)]
        + [pl.BlockSpec((count, META), lambda i: (0, meta_at))] * blocks
        + in_vmem(4),
        out_shape,
        in_vmem(len(out_shape)),
        deps,
        grid=(1,),
        name="route_sums",
    )


def plane_shift(value, near, name):
    count = lax.axis_size("exp")
    pairs = []
    for c in range(lax.axis_size("ctx")):
        for i in range(count):
            bits = 1 if (i % 2 == 0) == near else 2
            pairs.append((c * count + i, (c ^ bits) * count + i))
    with jax.named_scope(name):
        return lax.ppermute(value, ("ctx", "exp"), pairs)


class Chunk:
    def __init__(self, name, plan, weights, capacity, experts, mine):
        self.name, self.plan, self.weights, self.mine = name, plan, weights, mine
        self.capacity, self.experts = capacity, experts

    def multiply(self, tokens, *deps):
        return self.begin(
            tokens, *products(self.plan, tokens, *self.weights, self.capacity, self.experts, deps)
        )

    def begin(self, tokens, send, kept):
        self.tokens, self.kept = tokens, kept
        self.got = plane_shift(send, True, self.name + "_sums_near")
        return kept

    def add(self, *deps):
        half = add_parts([(self.got, 0), (self.kept, 0)], BF16, deps)
        self.other = plane_shift(half, False, self.name + "_sums_far")
        return half

    def turn(self, *deps):
        self.own = hidden_back(self.got, self.kept, self.other, deps)
        self.from_far = plane_shift(self.own, False, self.name + "_own_far")
        return self.own

    def forward(self, *deps):
        self.joined = join(self.own, self.from_far, deps)
        self.from_near = plane_shift(self.joined, True, self.name + "_both_near")
        return self.joined

    def finish(self, *deps):
        return route_sums(
            self.plan,
            self.tokens,
            self.mine,
            [self.joined, self.from_near],
            *self.weights[:2],
            self.capacity,
            self.experts,
            deps,
        )


def near_layers(
    moe_input, moe_grad, routes, gates, w_gate, w_up, w_down, queries, out_grad, positions, latents
):
    tok_rows = moe_input.shape[0]
    fanout = routes.shape[1]
    local = w_gate.shape[0]
    exp_count = lax.axis_size("exp")
    experts = local * exp_count
    capacity = tok_rows * fanout // experts * 5 // 4
    ctx, exp = lax.axis_index("ctx"), lax.axis_index("exp")
    x, y = ctx % 2, ctx // 2
    near = jnp.where(exp % 2 == 0, x, y)
    far = jnp.where(exp % 2 == 0, y, x)
    near_bit = jnp.where(exp % 2 == 0, 1, 2)
    plan = jnp.stack(
        [
            exp * local,
            (1 - near) * 2 + 1 - far,
            (1 - near) * 2 + far,
            near * 2 + 1 - far,
            near * 2 + far,
            near * 2 + far,
            near * 2 + 1 - far,
            (1 - near) * 2 + far,
            (1 - near) * 2 + 1 - far,
            exp,
            ctx,
            ctx ^ (3 - near_bit),
            ctx ^ near_bit,
            ctx ^ 3,
        ]
    ).astype(jnp.int32)

    def chunk(name, mine):
        return Chunk(name, plan, weights, capacity, experts, mine)

    own = pack_tokens(moe_input, moe_grad, routes, gates, experts)
    partner = shift(own, 1, "partner_move")
    first = [own, partner]
    LENGTH[0] = 10
    send, kept, *weights = first_products(plan, first, (w_gate, w_up, w_down), capacity, experts)
    a = chunk("a", 1)
    from_1 = shift(own, 2, "from_1_move")
    from_3 = shift(own, 6, "from_3_move")
    other_1 = shift(from_1, 1, "other_1_move")
    other_3 = shift(from_3, 1, "other_3_move")
    from_2 = shift(from_3, 2, "from_2_move")
    other_2 = shift(from_2, 1, "other_2_move")
    keys = latents.T
    keys_near = plane_shift(keys, True, "keys_near_move")
    keys_far = plane_shift(keys, False, "keys_far_move")
    keys_both = plane_shift(keys_near, False, "keys_both_move")
    made = {}

    def attend(*deps):
        made["queries"], give, made["keep"] = attention(
            plan, queries, out_grad, positions, [keys, keys_far, keys_near, keys_both], deps
        )
        made["got"] = shift(give, 1, "got_move")
        return made["keep"]

    def latent_cores(*deps):
        made["cores"] = both = add_parts([(made["keep"][None], 0), (made["got"][None], 0)], BF16, deps)
        made["terms"] = [shift(both[i], 2 * i, "latent_terms") for i in range(1, exp_count // 2)]
        return both

    def latent_chips(*deps):
        terms = [(made["cores"], 0)] + [(term[None], 0) for term in made["terms"]]
        made["chips"] = both = add_parts(terms, BF16, deps)
        made["crossed"] = plane_shift(both[2:], True, "crossed_move")
        return both

    def latent_near(*deps):
        terms = [(made["chips"][None, :2], 0), (made["crossed"][None], 0)]
        made["pair"] = both = add_parts(terms, BF16, deps)
        made["last"] = plane_shift(both[1], False, "last_move")
        return both

    def latent_far(*deps):
        terms = [(made["pair"], 0), (made["last"][None], 0)]
        made["latents"] = add_parts(terms, F32, deps)
        return made["latents"]

    def start_total(*deps):
        made["total"], theirs = a.finish(*deps)
        made["more"] = [(shift(theirs, 1, "a_other_move"), 0)]
        return theirs

    def finish(chunk):
        def act(*deps):
            *mine, theirs = chunk.finish(*deps)
            made[chunk.name] = mine
            made[chunk.name + "_other"] = shift(theirs, 1, chunk.name + "_other_move")
            return theirs

        return act

    def send_back(chunk, bits):
        def act(*deps):
            made[chunk.name + "_back"] = []
            for place, bit in enumerate(bits):
                terms = [(made[chunk.name][0], place), (made[chunk.name + "_other"], place)]
                both = add_parts(terms, BF16, deps)
                back = shift(both, bit, chunk.name + "_back_move")
                made[chunk.name + "_back"].append((back[None], 0))
            return both

        return act

    def receive(chunk, last):
        def act(*deps):
            terms = [(made["total"], 0)] + made.pop("more", []) + made[chunk.name + "_back"]
            total = add_parts(terms, BF16 if last else F32, deps)
            made["total"] = total[None]
            return total

        return act

    b = chunk("b", 1)
    c = chunk("c", 1)
    d = chunk("d", 1)
    order = (
        (functools.partial(b.multiply, [from_1, other_1]), 2),
        (a.add, 2),
        (a.turn, 2),
        (attend, 2),
        (a.forward, 2),
        (b.add, 2),
        (start_total, 2),
        (functools.partial(c.multiply, [from_3, other_3]), 2),
        (b.turn, 2, from_2),
        (latent_cores, 2, keys_both),
        (b.forward, 2),
        (c.add, 2),
        (functools.partial(d.multiply, [from_2, other_2]), 2),
        (finish(b), 2),
        (latent_chips, 2),
        (c.turn, 0),
        (send_back(b, (2,)), 2),
        (d.add, 2),
        (c.forward, 2),
        (latent_near, 2),
        (d.turn, 2),
        (finish(c), 2),
        (receive(b, False), 2),
        (d.forward, 2),
        (send_back(c, (6,)), 2),
        (latent_far, 2),
        (finish(d), 2),
        (receive(c, False), 2),
        (send_back(d, (4,)), 2),
        (receive(d, True), 2),
    )
    step = a.begin(first, send, kept)
    for act, length, *waits in order:
        LENGTH[0] = length
        step = act(step, *waits)
    return (made["total"][0], made["queries"], made["latents"])


def attention_kernel(heads, plan_ref, queries_ref, grads_ref, positions_ref, *refs):
    key_refs, (query_ref, give_ref, keep_ref, total_ref) = refs[:4], refs[4:]
    rows = queries_ref.shape[0]
    width, keys = key_refs[0].shape
    values = grads_ref.shape[1] // heads
    chips, shards, own_keys, _ = give_ref.shape
    square = lax.broadcasted_iota(jnp.int32, (rows, rows), 0)
    diagonal = square == lax.broadcasted_iota(jnp.int32, (rows, rows), 1)
    position = jnp.sum(
        jnp.where(diagonal, positions_ref[...].astype(F32), 0.0), axis=1, keepdims=True
    ).astype(jnp.int32)
    offset = lax.broadcasted_iota(jnp.int32, (rows, keys), 1)
    visible = [offset + plan_ref[10 + r] * keys <= position for r in range(shards)]
    outs = []
    for h in range(heads):
        query = queries_ref[:, h * width : (h + 1) * width]
        grad = grads_ref[:, h * values : (h + 1) * values]
        scores = [
            jnp.where(visible[r], dot(query, key_refs[r][...]) * SCORE_SCALE, MASKED)
            for r in range(shards)
        ]
        peak = functools.reduce(jnp.maximum, scores)
        peak = jnp.max(peak, axis=1, keepdims=True)
        raw = [jnp.where(visible[r], jnp.exp(scores[r] - peak), 0.0) for r in range(shards)]
        whole = jnp.sum(functools.reduce(jnp.add, raw), axis=1, keepdims=True)
        attend = [part / whole for part in raw]
        value_dot = [dot(grad, key_refs[r][:values, :]) for r in range(shards)]
        row_dot = functools.reduce(jnp.add, [a * v for a, v in zip(attend, value_dot)])
        row_dot = jnp.sum(row_dot, axis=1, keepdims=True)
        query_grad = None
        for r in range(shards):
            score_grad = (attend[r] * (value_dot[r] - row_dot)).astype(BF16)
            term = dot_t(score_grad, key_refs[r][...])
            query_grad = term if query_grad is None else query_grad + term
            key_grad = dot_rows(score_grad, query) * SCORE_SCALE
            value_grad = dot_rows(attend[r].astype(BF16), grad)
            part = pl.ds(r * keys, keys)
            if h == 0:
                total_ref[part, :] = key_grad
            else:
                total_ref[part, :] += key_grad
            total_ref[part, :values] += value_grad
        outs.append((query_grad * SCORE_SCALE).astype(BF16))
    query_ref[...] = jnp.concatenate(outs, axis=1)
    core, chip = plan_ref[9] % 2, plan_ref[9] // 2
    for b in range(chips):
        for r in range(shards):
            start = r * keys + (chip ^ b) * (2 * own_keys)
            across = (r % 2) * 2 + r // 2
            for out_ref, which, place in ((give_ref, 1 - core, across), (keep_ref, core, r)):
                at = pl.multiple_of(start + which * own_keys, own_keys)
                out_ref[b, place] = total_ref[pl.ds(at, own_keys), :].astype(BF16)


def dot_rows(left, right):
    return lax.dot_general(left, right, (((0,), (0,)), ((), ())), preferred_element_type=F32)


def attention(plan, queries, out_grad, positions, keys, deps):
    rows = queries.shape[0]
    width, count = keys[0].shape
    heads = queries.shape[1] // width
    exp_count = lax.axis_size("exp")
    terms = jax.ShapeDtypeStruct((exp_count // 2, len(keys), count // exp_count, width), BF16)
    return call(
        functools.partial(attention_kernel, heads),
        [plan, queries, out_grad, positions.reshape(1, rows), *keys],
        [pl.BlockSpec(memory_space=pltpu.SMEM)] + in_vmem(3 + len(keys)),
        [jax.ShapeDtypeStruct(queries.shape, BF16), terms, terms],
        in_vmem(3),
        deps,
        scratch=[pltpu.VMEM((len(keys) * count, width), F32)],
        name="attention",
    )


def far_expert_layer(moe_input, moe_grad, routes, gates, w_gate, w_up, w_down):
    tok_rows, width_part = moe_input.shape
    fanout = routes.shape[1]
    local_experts = w_gate.shape[0]
    exp_count = lax.axis_size("exp")
    experts = local_experts * exp_count
    capacity = tok_rows * fanout // experts * 5 // 4
    flat_routes = routes.reshape(-1)
    onehot = (flat_routes[:, None] == jnp.arange(experts, dtype=jnp.int32)[None, :]).astype(
        jnp.int32
    )
    before = jnp.cumsum(onehot, axis=0) - onehot
    slot_index = jnp.sum(before * onehot, axis=1)
    target = flat_routes * capacity + slot_index
    source_rows = jnp.arange(tok_rows * fanout, dtype=jnp.int32) // fanout
    empty = jnp.zeros((experts * capacity, width_part), BF16)
    send_shape = (exp_count, local_experts * capacity, width_part)
    send_input = empty.at[target].set(moe_input[source_rows]).reshape(send_shape)
    send_grad = empty.at[target].set(moe_grad[source_rows]).reshape(send_shape)
    recv_input, recv_grad = (
        lax.all_to_all(send_input, "exp", split_axis=0, concat_axis=0, tiled=True),
        lax.all_to_all(send_grad, "exp", split_axis=0, concat_axis=0, tiled=True),
    )
    slot_shape = (exp_count, local_experts, capacity, width_part)
    recv_input = recv_input.reshape(slot_shape)
    recv_grad = recv_grad.reshape(slot_shape)
    gate_part = jnp.einsum("sekd,edh->sekh", recv_input, w_gate, preferred_element_type=F32)
    up_part = jnp.einsum("sekd,edh->sekh", recv_input, w_up, preferred_element_type=F32)
    down_part = jnp.einsum("sekd,ehd->sekh", recv_grad, w_down, preferred_element_type=F32)
    gate_pre, up_pre, hidden_grad = (
        lax.psum(gate_part.astype(BF16), "ctx").astype(F32),
        lax.psum(up_part.astype(BF16), "ctx").astype(F32),
        lax.psum(down_part.astype(BF16), "ctx").astype(F32),
    )
    gate_back, up_back = swiglu_back(gate_pre, up_pre, hidden_grad)
    route_part = jnp.einsum("sekh,edh->sekd", gate_back, w_gate, preferred_element_type=F32)
    route_part = route_part + jnp.einsum(
        "sekh,edh->sekd", up_back, w_up, preferred_element_type=F32
    )
    route_part = route_part.astype(BF16).reshape(send_shape)
    returned = lax.all_to_all(route_part, "exp", split_axis=0, concat_axis=0, tiled=True).reshape(
        experts * capacity, width_part
    )
    per_route = returned[target].reshape(tok_rows, fanout, width_part).astype(F32)
    return jnp.sum(per_route * gates[:, :, None], axis=1).astype(BF16)


def sum_latent_grad(part):
    keys, width = part.shape
    shards, exp_count = lax.axis_size("ctx"), lax.axis_size("exp")
    part = part.reshape(shards, exp_count, keys // shards // exp_count, width).swapaxes(0, 1)
    part = part.reshape(keys, width).astype(BF16)
    part = lax.psum_scatter(part, "exp", scatter_dimension=0, tiled=True)
    return lax.psum_scatter(part.astype(F32), "ctx", scatter_dimension=0, tiled=True)


def attention_layer(queries, out_grad, positions, latents):
    q_rows = queries.shape[0]
    lat_width = latents.shape[1]
    head_count = queries.shape[1] // lat_width
    val_width = out_grad.shape[1] // head_count
    query_heads = queries.reshape(q_rows, head_count, lat_width)
    grad_heads = out_grad.reshape(q_rows, head_count, val_width)
    gathered = lax.all_gather(latents, "ctx", axis=0, tiled=True)
    key_ids = jnp.arange(gathered.shape[0], dtype=jnp.int32)
    visible = (key_ids[None, :] <= positions[:, None])[None]
    scores = (
        jnp.einsum("qhc,kc->hqk", query_heads, gathered, preferred_element_type=F32) * SCORE_SCALE
    )
    scores = jnp.where(visible, scores, MASKED)
    peak = jnp.max(scores, axis=2, keepdims=True)
    raw = jnp.where(visible, jnp.exp(scores - peak), 0.0)
    attend = raw / jnp.sum(raw, axis=2, keepdims=True)
    value_dot = jnp.einsum(
        "qhv,kv->hqk", grad_heads, gathered[:, :val_width], preferred_element_type=F32
    )
    row_dot = jnp.sum(attend * value_dot, axis=2, keepdims=True)
    score_grad = (attend * (value_dot - row_dot)).astype(BF16)
    query_grad = (
        jnp.einsum("hqk,kc->qhc", score_grad, gathered, preferred_element_type=F32) * SCORE_SCALE
    )
    key_grad = (
        jnp.einsum("hqk,qhc->kc", score_grad, query_heads, preferred_element_type=F32)
        * SCORE_SCALE
    )
    value_grad = jnp.einsum(
        "hqk,qhv->kv", attend.astype(BF16), grad_heads, preferred_element_type=F32
    )
    latent_part = key_grad + jnp.pad(value_grad, ((0, 0), (0, lat_width - val_width)))
    latent_grad = sum_latent_grad(latent_part)
    query_out = query_grad.astype(BF16).reshape(q_rows, head_count * lat_width)
    return (query_out, latent_grad)


def per_device(
    moe_input, moe_grad, routes, gates, w_gate, w_up, w_down, queries, out_grad, positions, latents
):
    if lax.axis_size("exp") <= routes.shape[1]:
        return near_layers(
            moe_input, moe_grad, routes, gates, w_gate, w_up, w_down,
            queries, out_grad, positions, latents,
        )
    query_out, latent_grad = attention_layer(queries, out_grad, positions, latents)
    input_grad = far_expert_layer(moe_input, moe_grad, routes, gates, w_gate, w_up, w_down)
    return (input_grad, query_out, latent_grad)


def solution(mesh):
    return jax.shard_map(
        per_device,
        mesh=mesh,
        in_specs=(
            P("exp", "ctx"),
            P("exp", "ctx"),
            P("exp", None),
            P("exp", None),
            P("exp", "ctx", None),
            P("exp", "ctx", None),
            P("exp", None, "ctx"),
            P("ctx", "exp"),
            P("ctx", "exp"),
            P("ctx"),
            P("ctx", None),
        ),
        out_specs=(P("exp", "ctx"), P("ctx", "exp"), P(("ctx", "exp"), None)),
        check_vma=False,
    )
```
